512 devices in a mesh: expert: 16 (over x, y), tensor: 32 (over z, core).
Axes of the slice: x: 4, y: 4, z: 16, core: 2. Of those that a mesh axis runs over, the one named last changes fastest.
Arguments:
- query: bfloat16 [2048, 4096], P('tensor', 'expert'), may hold values from -140 to 140
- keys: bfloat16 [2048, 1024], P('tensor'), may hold values from -6 to 6
- values: bfloat16 [2048, 1024], P('tensor'), may hold values from -6 to 6
- resid: bfloat16 [2048, 4096], P('tensor', 'expert'), may hold values from -16 to 16
- route_ids: int32 [2048, 4], P('tensor'), may hold values from 0 to 15, all different within a row; in each aligned block of 64 rows (0 to 63, 64 to 127, ...) at most 32 rows name the same one
- route_weight: float32 [2048, 4], P('tensor'), may hold values from 0.1 to 1
- w_in: bfloat16 [16, 4096, 8192], P('expert', None, 'tensor'), may hold values from -0.09375 to 0.09375
- expert_down_matrix: bfloat16 [16, 8192, 4096], P('expert', 'tensor'), may hold values from -0.0625 to 0.0625
Outputs:
- mixed: bfloat16 [2048, 4096], P('tensor', 'expert')
The draws below stay inside these ranges and needn't reach their ends.
Inputs may be any that keep to these rules, and one draw needn't show every extreme that they name: `route_ids`: each token names 4 different experts. In each aligned block of 64 positions no expert is named by more than 32 of them, and some expert reaches 32 in some block.
All inputs are finite; a program needn't handle non-finite values.
Results may differ from the reference program's by a relative error of at most 0.014.
Values may be sent and summed in bfloat16 or wider, within the bound.
No kernel may reach another device: no remote copies, remote signals or barrier semaphores. Data moves between devices by JAX's collectives and lax.ppermute only.
A program may use at most 64 MiB of HBM per device.

```python
import math
import jax
import jax.numpy as jnp
import numpy as np
from jax import lax

D = 4096
HEADS = 32
KV_HEADS = 8
HEAD_DIM = 128
FF = 8192
EXPERTS = 16
TOPK = 4
SPAN = 64
LEN = 2048
EXP_CAP = 32
N_TENSOR = 32


def shared_keys(key):
    return jnp.clip(jax.random.normal(key, (LEN, KV_HEADS * HEAD_DIM), jnp.float32), -6.0, 6.0)


def draw_keys(key, part):
    base = shared_keys(key)
    return base.astype(jnp.bfloat16)


def draw_query(key, part):
    key = jax.random.fold_in(key, 12)
    drawn = jnp.clip(jax.random.normal(key, (LEN, HEADS * HEAD_DIM), jnp.float32), -6.0, 6.0)
    return drawn.astype(jnp.bfloat16)


def draw_resid(key, part):
    key = jax.random.fold_in(key, 13)
    row_key, col_key, main_key = jax.random.split(key, 3)
    upper = math.log(10.0)
    values_base = jnp.clip(jax.random.normal(main_key, (LEN, D), jnp.float32), -4.0, 4.0)
    row_scale = 0.2 * jnp.exp(jax.random.uniform(row_key, (LEN, 1), jnp.float32, 0.0, upper))
    col_scale = 0.2 * jnp.exp(jax.random.uniform(col_key, (1, D), jnp.float32, 0.0, upper))
    return jnp.clip(values_base * row_scale * col_scale, -16.0, 16.0).astype(jnp.bfloat16)


def levels(rng, extent, cuts, smallest, largest):
    def one(position, shards_of):
        steps = jax.random.uniform(jax.random.fold_in(jax.random.fold_in(rng, 6), position), (shards_of,), jnp.float32, smallest / len(cuts), largest / len(cuts))
        return jnp.repeat(jnp.exp(steps), extent[position] // shards_of).reshape((-1,) + (1,) * (len(extent) - position - 1))

    level = one(*cuts[0])
    for cut in cuts[1:]:
        level = level * one(*cut)
    return level


def assign_block(stream_key, own, number, rows, number_of, top, limit, slope):
    ranking = jax.random.permutation(stream_key, number_of)
    packed, usual = load_shares(number_of, rows * top, limit, slope, True), load_shares(number_of, rows * top, limit, slope, False)
    places = jnp.arange(number_of)

    def named(lengths, offset_by):
        used = int((lengths > 0).sum())
        fixed = max(1, used // 4)
        passed = fixed + (places - fixed + offset_by * (used - fixed)) % max(1, number_of - fixed)
        return jnp.zeros((number_of,), jnp.int32).at[ranking[jnp.where(places < fixed, places, passed)]].set(jnp.asarray(lengths, jnp.int32))

    lengths = jnp.where(number % 4 == 0, named(packed, number // 4), named(usual, number - number // 4 - 1))
    mixed = jax.random.permutation(jax.random.fold_in(own, 3), number_of)
    giver, sink = mixed[0:number_of // 2 * 2:2], mixed[1:number_of // 2 * 2:2]
    room = jnp.minimum(lengths[giver] - 1, limit - lengths[sink]) // 2
    room = jnp.where((giver == ranking[0]) | (sink == ranking[0]) | (lengths[sink] == 0), 0, jnp.maximum(room, 0))
    passed = jax.random.randint(jax.random.fold_in(own, 4), (number_of // 2,), 0, 1 << 20) % (room + 1)
    lengths = lengths.at[giver].add(-passed).at[sink].add(passed)
    items = jnp.searchsorted(jnp.cumsum(lengths), jnp.arange(rows * top), side="right").astype(jnp.int32)
    listing = items.reshape(top, rows).T
    listing = listing[jax.random.permutation(jax.random.fold_in(own, 1), rows)]
    offset_by = jax.random.randint(jax.random.fold_in(own, 2), (rows, 1), 0, top)
    return jnp.take_along_axis(listing, (jnp.arange(top)[None, :] + offset_by) % top, axis=1)


def load_shares(number_of, total, reach, skew, full):
    weights = [(1 << 20) // math.isqrt(rank ** skew) + 1 for rank in range(1, number_of + 1)]
    largest = reach if full else min(reach, max(-(-total // number_of), total * weights[0] // sum(weights)))
    least = 1 if total - largest >= number_of - 1 else 0
    given, surplus = [largest] + [least] * (number_of - 1), total - largest - least * (number_of - 1)
    while surplus > 0:
        free = [i for i in range(1, number_of) if given[i] < largest] or [i for i in range(1, number_of) if given[i] < reach]
        mass, left = sum([weights[i] for i in free]), surplus
        for i in free:
            extra = min(reach - given[i], max(1, left * weights[i] // mass), surplus)
            given[i] = given[i] + extra
            surplus = surplus - extra
    return np.array(given)


def centred(own_key, dims, scale, most, pieces=(), kind=jnp.bfloat16):
    array = scale * jax.random.normal(own_key, dims, jnp.float32)
    if pieces:
        array = array * levels(own_key, dims, pieces, -0.22, 0.18)
    return jnp.clip(array, -most, most).astype(kind)


def setup_inputs(seed: int = 0) -> dict:
    seeds = jax.random.split(jax.random.key(seed), 9)
    query = draw_query(jax.random.fold_in(seeds[8], 71), 0)
    keys = draw_keys(jax.random.fold_in(seeds[8], 71), 0)
    values = centred(seeds[2], (LEN, KV_HEADS * HEAD_DIM), 1.0, 6.0, ((0, 32),))
    resid = draw_resid(jax.random.fold_in(seeds[8], 71), 0)
    route_ids_keys = jax.random.split(jax.random.fold_in(seeds[4], 1), LEN // SPAN)
    route_ids_turns = jax.random.permutation(jax.random.fold_in(seeds[4], 3), LEN // SPAN)
    route_ids = jax.vmap(lambda own, number: assign_block(jax.random.fold_in(seeds[4], 2), own, number, SPAN, EXPERTS, TOPK, EXP_CAP, 2))(route_ids_keys, route_ids_turns).reshape((LEN, TOPK))
    route_weight = jnp.clip(jnp.exp(math.log(1.0) - 2.3025851 * jax.random.uniform(seeds[5], (LEN, TOPK), jnp.float32) ** levels(seeds[5], (LEN, TOPK), ((0, 32),), -0.2, 0.2)), 0.1, 1.0)
    w_in = centred(seeds[6], (EXPERTS, D, FF), D ** -0.5, 0.09375, ((0, 16), (2, 32)))
    expert_down_matrix = centred(seeds[7], (EXPERTS, FF, D), FF ** -0.5, 0.0625, ((0, 16), (1, 32)))
    return {"query": query, "keys": keys, "values": values, "resid": resid, "route_ids": route_ids, "route_weight": route_weight, "w_in": w_in, "expert_down_matrix": expert_down_matrix}


def reference(query, keys, values, resid, route_ids, route_weight, w_in, expert_down_matrix):
    group_size = HEADS // KV_HEADS
    query_heads = query.astype(jnp.float32).reshape(LEN, HEADS, HEAD_DIM)
    key_heads = jnp.repeat(keys.astype(jnp.float32).reshape(LEN, KV_HEADS, HEAD_DIM), group_size, axis=1)
    value_heads = jnp.repeat(values.astype(jnp.float32).reshape(LEN, KV_HEADS, HEAD_DIM), group_size, axis=1)
    scores = jnp.einsum('qhd,khd->hqk', query_heads, key_heads) / math.sqrt(HEAD_DIM)
    causal = jnp.arange(LEN)[:, None] >= jnp.arange(LEN)[None, :]
    scores = jnp.where(causal[None], scores, -1e+30)
    top_score = lax.optimization_barrier(jnp.max(scores, axis=-1, keepdims=True))
    raised = jnp.exp(scores - top_score)
    shares = raised / lax.optimization_barrier(jnp.sum(raised, axis=-1, keepdims=True))
    probs = lax.optimization_barrier(shares.astype(jnp.bfloat16)).astype(jnp.float32)
    attended = jnp.einsum('hqk,khd->qhd', probs, value_heads).reshape(LEN, D)
    state = (resid.astype(jnp.float32) + attended).astype(jnp.bfloat16)
    state_wide = state.astype(jnp.float32)
    center = lax.optimization_barrier(jnp.mean(state_wide, axis=1, keepdims=True))
    variance = lax.optimization_barrier(jnp.mean((state_wide - center) ** 2, axis=1, keepdims=True))
    normed = ((state_wide - center) * lax.rsqrt(variance + 1e-05)).astype(jnp.bfloat16)
    route_norm = route_weight / lax.optimization_barrier(jnp.sum(route_weight, axis=1, keepdims=True))
    expert_grid = jnp.arange(EXPERTS, dtype=jnp.int32)
    picked = route_ids[:, :, None] == expert_grid[None, None, :]
    gate_table = lax.optimization_barrier(jnp.sum(jnp.where(picked, route_norm[:, :, None], 0.0), axis=1))
    live_table = jnp.any(picked, axis=1)

    def run_expert(index):
        live_rows = lax.dynamic_index_in_dim(live_table, index, 1, keepdims=False)
        rows_in = jnp.where(live_rows[:, None], normed, jnp.zeros_like(normed))
        hidden_activation = jax.nn.silu(jnp.dot(rows_in, w_in[index], preferred_element_type=jnp.float32)).astype(jnp.bfloat16)
        hidden_sharding_plan = hidden_activation.astype(jnp.float32).reshape(LEN, N_TENSOR, FF // N_TENSOR)
        result_sharding_plan = expert_down_matrix[index].astype(jnp.float32).reshape(N_TENSOR, FF // N_TENSOR, D)
        incomplete_summands = jnp.einsum('kir,irp->kip', hidden_sharding_plan, result_sharding_plan)
        quantized_copy = lax.optimization_barrier(incomplete_summands.astype(jnp.bfloat16)).astype(jnp.float32)
        return lax.optimization_barrier(jnp.sum(quantized_copy, axis=1)).astype(jnp.bfloat16)
    expert_outs = lax.map(run_expert, jnp.arange(EXPERTS, dtype=jnp.int32))
    mixture = jnp.einsum('le,eld->ld', gate_table, expert_outs.astype(jnp.float32))
    return (state_wide + mixture).astype(jnp.bfloat16)
```

```python
import math

import jax
import jax.numpy as jnp
from jax import lax
from jax.sharding import Mesh
from jax.sharding import PartitionSpec as P

HEADS = 32
KV_HEADS = 8
HEAD_DIM = 128
EXPERTS = 16
EXP_CAP = 32
TOPK = 4

E = ("x", "y")
T = ("z", "core")


def gather_kv(keys, values):
    place = lax.axis_index(E)
    group = place // 2
    odd = (place % 2) == 1
    k = lax.dynamic_slice_in_dim(keys, group * HEAD_DIM, HEAD_DIM, 1)
    v = lax.dynamic_slice_in_dim(values, group * HEAD_DIM, HEAD_DIM, 1)
    mine = lax.all_gather(jnp.where(odd, v, k), T, axis=0, tiled=True)
    other = lax.ppermute(mine, "y", [(0, 1), (1, 0), (2, 3), (3, 2)])
    return jnp.where(odd, other, mine), jnp.where(odd, mine, other)


def attend(query, k, v, tensor_place):
    block = query.shape[0]
    heads = query.shape[1] // HEAD_DIM
    total = k.shape[0]
    q = query.reshape(block, heads, HEAD_DIM)
    scores = jnp.einsum("qhd,kd->hqk", q, k, preferred_element_type=jnp.float32)
    scores = scores / math.sqrt(HEAD_DIM)
    query_pos = tensor_place * block + jnp.arange(block)
    causal = query_pos[:, None] >= jnp.arange(total)[None, :]
    scores = jnp.where(causal[None], scores, -1e30)
    top = jnp.max(scores, axis=-1, keepdims=True)
    raised = jnp.exp(scores - top)
    probs = (raised / jnp.sum(raised, axis=-1, keepdims=True)).astype(jnp.bfloat16)
    out = jnp.einsum("hqk,kd->qhd", probs, v, preferred_element_type=jnp.float32)
    return out.reshape(block, heads * HEAD_DIM)


def slots_of(ids):
    grid = jnp.arange(EXPERTS, dtype=jnp.int32)
    picked = ids[:, :, None] == grid[None, None, :]
    chosen = jnp.any(picked, axis=1)
    rows = ids.shape[0]
    lower = (jnp.arange(rows)[:, None] > jnp.arange(rows)[None, :]).astype(jnp.bfloat16)
    rank = jnp.dot(lower, chosen.astype(jnp.bfloat16), preferred_element_type=jnp.float32).astype(jnp.int32)
    rank_of = jnp.sum(jnp.where(picked, rank[:, None, :], 0), axis=2)
    return ids * EXP_CAP + rank_of


def per_device(query, keys, values, resid, route_ids, route_weight, w_in, w_down):
    tensor_place = lax.axis_index(T)
    core = lax.axis_index("core")
    block, width = query.shape
    k, v = gather_kv(keys, values)
    attended = attend(query, k, v, tensor_place)
    state = (resid.astype(jnp.float32) + attended).astype(jnp.bfloat16)

    slots = slots_of(route_ids)
    slot_grid = jnp.arange(EXPERTS * EXP_CAP, dtype=jnp.int32)
    takes = (slots[:, :, None] == slot_grid[None, None, :]).astype(jnp.bfloat16)
    sent = jnp.einsum("tps,td->sd", takes, state, preferred_element_type=jnp.float32).astype(jnp.bfloat16)
    rows = lax.all_to_all(
        sent.reshape(EXPERTS, EXP_CAP, width), E, split_axis=0, concat_axis=0, tiled=True
    )
    rows = rows.transpose(1, 0, 2).reshape(EXP_CAP, EXPERTS * width)
    wide = rows.astype(jnp.float32)
    center = jnp.mean(wide, axis=1, keepdims=True)
    variance = jnp.mean((wide - center) ** 2, axis=1, keepdims=True)
    normed = ((wide - center) * lax.rsqrt(variance + 1e-05)).astype(jnp.bfloat16)

    tokens = lax.all_gather(normed, T, axis=0, tiled=True)
    hidden = jnp.dot(tokens, w_in[0], preferred_element_type=jnp.float32)
    hidden = jax.nn.silu(hidden).astype(jnp.bfloat16)
    hidden = hidden.reshape(-1, 2, EXP_CAP, hidden.shape[1])
    z_count = hidden.shape[0]
    theirs = lax.dynamic_index_in_dim(hidden, 1 - core, 1, keepdims=False)
    ours = lax.dynamic_index_in_dim(hidden, core, 1, keepdims=False)
    theirs = theirs.reshape(z_count * EXP_CAP, -1)
    ours = ours.reshape(z_count * EXP_CAP, -1)
    away = jnp.dot(theirs, w_down[0], preferred_element_type=jnp.float32).astype(jnp.bfloat16)
    came = lax.ppermute(away, "core", [(0, 1), (1, 0)])
    here = jnp.dot(ours, w_down[0], preferred_element_type=jnp.float32)
    pair = (here + came.astype(jnp.float32)).astype(jnp.bfloat16)
    summed = lax.psum_scatter(pair, "z", scatter_dimension=0, tiled=True)

    back = summed.reshape(EXP_CAP, EXPERTS, width).transpose(1, 0, 2)
    back = lax.all_to_all(back, E, split_axis=0, concat_axis=0, tiled=True)
    back = back.reshape(EXPERTS * EXP_CAP, width)
    outs = jnp.einsum("tps,sd->tpd", takes, back, preferred_element_type=jnp.float32)
    gates = route_weight / jnp.sum(route_weight, axis=1, keepdims=True)
    mixture = jnp.sum(gates[:, :, None] * outs, axis=1)
    return (state.astype(jnp.float32) + mixture).astype(jnp.bfloat16)


def solution(mesh):
    fine = Mesh(mesh.devices.reshape(4, 4, 16, 2), ("x", "y", "z", "core"))
    placed = (
        P(T, E),
        P(T, None),
        P(T, None),
        P(T, E),
        P(T, None),
        P(T, None),
        P(E, None, T),
        P(E, T, None),
    )
    return jax.shard_map(per_device, mesh=fine, in_specs=placed, out_specs=P(T, E), check_vma=False)
```

```python
import math

import jax
import jax.numpy as jnp
from jax import lax
from jax.sharding import Mesh
from jax.sharding import PartitionSpec as P

HEADS = 32
KV_HEADS = 8
HEAD_DIM = 128
EXPERTS = 16
EXP_CAP = 32
TOPK = 4
Z = 16

E = ("x", "y")
T = ("z", "core")


def swap_cores(x):
    return lax.ppermute(x, "core", [(0, 1), (1, 0)])


def gather_kv(keys, values):
    group = lax.axis_index(E) // 2
    core = lax.axis_index("core")
    k = lax.dynamic_slice_in_dim(keys, group * HEAD_DIM, HEAD_DIM, 1)
    v = lax.dynamic_slice_in_dim(values, group * HEAD_DIM, HEAD_DIM, 1)
    first = core == 0
    came = swap_cores(jnp.where(first, v, k))
    kept = jnp.where(first, k, v)
    chip = jnp.concatenate([jnp.where(first, kept, came), jnp.where(first, came, kept)], axis=0)
    mine = lax.all_gather(chip, "z", axis=0, tiled=True)
    other = swap_cores(mine)
    return jnp.where(first, mine, other), jnp.where(first, other, mine)


def up(x):
    return lax.ppermute(x, "z", [(i, (i + 1) % Z) for i in range(Z)])


def down(x):
    return lax.ppermute(x, "z", [((i + 1) % Z, i) for i in range(Z)])


def experts(normed, w_in, w_down):
    w_in = lax.all_gather(w_in, "core", axis=0, tiled=True)
    w_down = lax.all_gather(w_down, "core", axis=0, tiled=True)

    def share(blocks):
        rows = jnp.concatenate(blocks, axis=0)
        hidden = jnp.einsum("rd,cdf->rcf", rows, w_in, preferred_element_type=jnp.float32)
        hidden = jax.nn.silu(hidden).astype(jnp.bfloat16)
        out = jnp.einsum("rcf,cfd->rd", hidden, w_down, preferred_element_type=jnp.float32)
        out = out.astype(jnp.bfloat16)
        return [out[i * EXP_CAP : (i + 1) * EXP_CAP] for i in range(len(blocks))]

    above, below = Z // 2, Z // 2 - 1
    from_below, from_above = [normed], [normed]
    for _ in range(above):
        from_below.append(up(from_below[-1]))
        if len(from_above) <= below:
            from_above.append(down(from_above[-1]))
    half = above // 2
    near = from_below[: half + 1] + from_above[1:half]
    far = from_below[half + 1 :] + from_above[half:]
    near, far = share(near), share(far)
    sums_below = near[: half + 1] + far[: above - half]
    sums_above = near[:1] + near[half + 1 :] + far[above - half :]

    def add(a, b):
        return (a.astype(jnp.float32) + b.astype(jnp.float32)).astype(jnp.bfloat16)

    low, high = sums_below[above], sums_above[below]
    for i in range(1, above + 1):
        low = down(low)
        if i < above:
            low = add(low, sums_below[above - i])
        if i <= below:
            high = up(high)
            if i < below:
                high = add(high, sums_above[below - i])
    total = near[0].astype(jnp.float32) + low.astype(jnp.float32) + high.astype(jnp.float32)
    return total.astype(jnp.bfloat16)


def attend(query, k, v, tensor_place):
    block = query.shape[0]
    heads = query.shape[1] // HEAD_DIM
    total = k.shape[0]
    q = query.reshape(block, heads, HEAD_DIM)
    scores = jnp.einsum("qhd,kd->hqk", q, k, preferred_element_type=jnp.float32)
    scores = scores / math.sqrt(HEAD_DIM)
    query_pos = tensor_place * block + jnp.arange(block)
    causal = query_pos[:, None] >= jnp.arange(total)[None, :]
    scores = jnp.where(causal[None], scores, -1e30)
    top = jnp.max(scores, axis=-1, keepdims=True)
    raised = jnp.exp(scores - top)
    probs = (raised / jnp.sum(raised, axis=-1, keepdims=True)).astype(jnp.bfloat16)
    out = jnp.einsum("hqk,kd->qhd", probs, v, preferred_element_type=jnp.float32)
    return out.reshape(block, heads * HEAD_DIM)


def slots_of(ids):
    grid = jnp.arange(EXPERTS, dtype=jnp.int32)
    picked = ids[:, :, None] == grid[None, None, :]
    chosen = jnp.any(picked, axis=1)
    rows = ids.shape[0]
    lower = (jnp.arange(rows)[:, None] > jnp.arange(rows)[None, :]).astype(jnp.bfloat16)
    rank = jnp.dot(lower, chosen.astype(jnp.bfloat16), preferred_element_type=jnp.float32).astype(jnp.int32)
    rank_of = jnp.sum(jnp.where(picked, rank[:, None, :], 0), axis=2)
    return ids * EXP_CAP + rank_of


def per_device(query, keys, values, resid, route_ids, route_weight, w_in, w_down):
    tensor_place = lax.axis_index(T)
    block, width = query.shape
    k, v = gather_kv(keys, values)
    attended = attend(query, k, v, tensor_place)
    state = (resid.astype(jnp.float32) + attended).astype(jnp.bfloat16)

    slots = slots_of(route_ids)
    slot_grid = jnp.arange(EXPERTS * EXP_CAP, dtype=jnp.int32)
    takes = (slots[:, :, None] == slot_grid[None, None, :]).astype(jnp.bfloat16)
    sent = jnp.einsum("tps,td->sd", takes, state, preferred_element_type=jnp.float32).astype(jnp.bfloat16)
    rows = lax.all_to_all(
        sent.reshape(EXPERTS, EXP_CAP, width), E, split_axis=0, concat_axis=0, tiled=True
    )
    rows = rows.transpose(1, 0, 2).reshape(EXP_CAP, EXPERTS * width)
    wide = rows.astype(jnp.float32)
    center = jnp.mean(wide, axis=1, keepdims=True)
    variance = jnp.mean((wide - center) ** 2, axis=1, keepdims=True)
    normed = ((wide - center) * lax.rsqrt(variance + 1e-05)).astype(jnp.bfloat16)

    summed = experts(normed, w_in, w_down)

    back = summed.reshape(EXP_CAP, EXPERTS, width).transpose(1, 0, 2)
    back = lax.all_to_all(back, E, split_axis=0, concat_axis=0, tiled=True)
    back = back.reshape(EXPERTS * EXP_CAP, width)
    outs = jnp.einsum("tps,sd->tpd", takes, back, preferred_element_type=jnp.float32)
    gates = route_weight / jnp.sum(route_weight, axis=1, keepdims=True)
    mixture = jnp.sum(gates[:, :, None] * outs, axis=1)
    return (state.astype(jnp.float32) + mixture).astype(jnp.bfloat16)


def solution(mesh):
    fine = Mesh(mesh.devices.reshape(4, 4, 16, 2), ("x", "y", "z", "core"))
    placed = (
        P(T, E),
        P(T, None),
        P(T, None),
        P(T, E),
        P(T, None),
        P(T, None),
        P(E, None, T),
        P(E, T, None),
    )
    return jax.shard_map(per_device, mesh=fine, in_specs=placed, out_specs=P(T, E), check_vma=False)
```

```python
import math

import jax
import jax.numpy as jnp
from jax import lax
from jax.sharding import Mesh
from jax.sharding import PartitionSpec as P

HEADS = 32
KV_HEADS = 8
HEAD_DIM = 128
EXPERTS = 16
EXP_CAP = 32
TOPK = 4

E = ("x", "y")
T = ("z", "core")


def swap_cores(x):
    return lax.ppermute(x, "core", [(0, 1), (1, 0)])


def gather_kv(keys, values):
    group = lax.axis_index(E) // 2
    core = lax.axis_index("core")
    k = lax.dynamic_slice_in_dim(keys, group * HEAD_DIM, HEAD_DIM, 1)
    v = lax.dynamic_slice_in_dim(values, group * HEAD_DIM, HEAD_DIM, 1)
    first = core == 0
    came = swap_cores(jnp.where(first, v, k))
    kept = jnp.where(first, k, v)
    chip = jnp.concatenate([jnp.where(first, kept, came), jnp.where(first, came, kept)], axis=0)
    mine = lax.all_gather(chip, "z", axis=0, tiled=True)
    other = swap_cores(mine)
    return jnp.where(first, mine, other), jnp.where(first, other, mine)


def experts(normed, w_in, w_down):
    w_in = lax.all_gather(w_in, "core", axis=0, tiled=True)
    w_down = lax.all_gather(w_down, "core", axis=0, tiled=True)
    rows = lax.all_gather(normed, "z", axis=0, tiled=True)
    hidden = jnp.einsum("rd,cdf->rcf", rows, w_in, preferred_element_type=jnp.float32)
    hidden = jax.nn.silu(hidden).astype(jnp.bfloat16)
    out = jnp.einsum("rcf,cfd->rd", hidden, w_down, preferred_element_type=jnp.float32)
    return lax.psum_scatter(out.astype(jnp.bfloat16), "z", scatter_dimension=0, tiled=True)


def attend(query, k, v, tensor_place):
    block = query.shape[0]
    heads = query.shape[1] // HEAD_DIM
    total = k.shape[0]
    q = query.reshape(block, heads, HEAD_DIM)
    scores = jnp.einsum("qhd,kd->hqk", q, k, preferred_element_type=jnp.float32)
    scores = scores / math.sqrt(HEAD_DIM)
    query_pos = tensor_place * block + jnp.arange(block)
    causal = query_pos[:, None] >= jnp.arange(total)[None, :]
    scores = jnp.where(causal[None], scores, -1e30)
    top = jnp.max(scores, axis=-1, keepdims=True)
    raised = jnp.exp(scores - top)
    probs = (raised / jnp.sum(raised, axis=-1, keepdims=True)).astype(jnp.bfloat16)
    out = jnp.einsum("hqk,kd->qhd", probs, v, preferred_element_type=jnp.float32)
    return out.reshape(block, heads * HEAD_DIM)


def slots_of(ids):
    grid = jnp.arange(EXPERTS, dtype=jnp.int32)
    picked = ids[:, :, None] == grid[None, None, :]
    chosen = jnp.any(picked, axis=1)
    rows = ids.shape[0]
    lower = (jnp.arange(rows)[:, None] > jnp.arange(rows)[None, :]).astype(jnp.bfloat16)
    rank = jnp.dot(lower, chosen.astype(jnp.bfloat16), preferred_element_type=jnp.float32).astype(jnp.int32)
    rank_of = jnp.sum(jnp.where(picked, rank[:, None, :], 0), axis=2)
    return ids * EXP_CAP + rank_of


def per_device(query, keys, values, resid, route_ids, route_weight, w_in, w_down):
    tensor_place = lax.axis_index(T)
    block, width = query.shape
    k, v = gather_kv(keys, values)
    attended = attend(query, k, v, tensor_place)
    state = (resid.astype(jnp.float32) + attended).astype(jnp.bfloat16)

    slots = slots_of(route_ids)
    slot_grid = jnp.arange(EXPERTS * EXP_CAP, dtype=jnp.int32)
    takes = (slots[:, :, None] == slot_grid[None, None, :]).astype(jnp.bfloat16)
    sent = jnp.einsum("tps,td->sd", takes, state, preferred_element_type=jnp.float32).astype(jnp.bfloat16)
    rows = lax.all_to_all(
        sent.reshape(EXPERTS, EXP_CAP, width), E, split_axis=0, concat_axis=0, tiled=True
    )
    rows = rows.transpose(1, 0, 2).reshape(EXP_CAP, EXPERTS * width)
    wide = rows.astype(jnp.float32)
    center = jnp.mean(wide, axis=1, keepdims=True)
    variance = jnp.mean((wide - center) ** 2, axis=1, keepdims=True)
    normed = ((wide - center) * lax.rsqrt(variance + 1e-05)).astype(jnp.bfloat16)

    summed = experts(normed, w_in, w_down)

    back = summed.reshape(EXP_CAP, EXPERTS, width).transpose(1, 0, 2)
    back = lax.all_to_all(back, E, split_axis=0, concat_axis=0, tiled=True)
    back = back.reshape(EXPERTS * EXP_CAP, width)
    outs = jnp.einsum("tps,sd->tpd", takes, back, preferred_element_type=jnp.float32)
    gates = route_weight / jnp.sum(route_weight, axis=1, keepdims=True)
    mixture = jnp.sum(gates[:, :, None] * outs, axis=1)
    return (state.astype(jnp.float32) + mixture).astype(jnp.bfloat16)


def solution(mesh):
    fine = Mesh(mesh.devices.reshape(4, 4, 16, 2), ("x", "y", "z", "core"))
    placed = (
        P(T, E),
        P(T, None),
        P(T, None),
        P(T, E),
        P(T, None),
        P(T, None),
        P(E, None, T),
        P(E, T, None),
    )
    return jax.shard_map(per_device, mesh=fine, in_specs=placed, out_specs=P(T, E), check_vma=False)
```

```python
import math

import jax
import jax.numpy as jnp
from jax import lax
from jax.experimental import pallas as pl
from jax.experimental.pallas import tpu as pltpu
from jax.sharding import Mesh
from jax.sharding import PartitionSpec as P

HEADS = 32
KV_HEADS = 8
HEAD_DIM = 128
EXPERTS = 16
EXP_CAP = 32
TOPK = 4
BLOCK = 64
HALF = 128
Z = 16
MIB = 1 << 20

E = ("x", "y")
T = ("z", "core")


def swap_cores(x):
    return lax.ppermute(x, "core", [(0, 1), (1, 0)])


def gather_kv(keys, values, notes):
    group = lax.axis_index(E) // 2
    core = lax.axis_index("core")
    k = lax.dynamic_slice_in_dim(keys, group * HEAD_DIM, HEAD_DIM, 1)
    v = lax.dynamic_slice_in_dim(values, group * HEAD_DIM, HEAD_DIM, 1)
    first = core == 0
    came = swap_cores(jnp.where(first, v, k))
    kept = jnp.where(first, k, v)
    chip = jnp.concatenate([jnp.where(first, kept, came), jnp.where(first, came, kept), notes], axis=0)
    all_chips = lax.all_gather(chip, "z", axis=0)
    mine = all_chips[:, : 2 * BLOCK].reshape(-1, HEAD_DIM)
    other = swap_cores(mine)
    return jnp.where(first, mine, other), jnp.where(first, other, mine), all_chips[:, 2 * BLOCK :]


def notes_of(ids, ranks, gates):
    top = lax.reduce_precision(gates, 8, 7)
    rest = gates - top
    middle = lax.reduce_precision(rest, 8, 7)
    low = rest - middle
    parts = [ids.astype(jnp.float32), ranks.astype(jnp.float32), top, middle, low]
    rows = jnp.concatenate([p.T.reshape(2, 128) for p in parts], axis=0).astype(jnp.bfloat16)
    return jnp.pad(rows, ((0, 6), (0, 0)))


def read_notes(notes):
    rows = notes[:, :10].astype(jnp.float32).reshape(Z, 5, TOPK, BLOCK)
    return rows[:, 0] * EXP_CAP + rows[:, 1], rows[:, 2] + rows[:, 3] + rows[:, 4]


def place_kernel(slots_ref, rows_ref, out_ref):
    for z in range(slots_ref.shape[0]):
        grid = lax.broadcasted_iota(jnp.int32, (EXPERTS * EXP_CAP, BLOCK), 0).astype(jnp.float32)
        hit = grid == slots_ref[z, 0:1, :]
        for p in range(1, TOPK):
            hit = jnp.logical_or(hit, grid == slots_ref[z, p : p + 1, :])
        take = jnp.where(hit, 1.0, 0.0).astype(jnp.bfloat16)
        out = jnp.dot(take, rows_ref[z], preferred_element_type=jnp.float32).astype(jnp.bfloat16)
        out_ref[:, z] = out.reshape(EXPERTS, EXP_CAP, HALF)


def place_rows(slots, rows):
    step = 8
    return pl.pallas_call(
        place_kernel,
        grid=(Z // step,),
        in_specs=[
            pl.BlockSpec((step, TOPK, BLOCK), lambda i: (i, 0, 0)),
            pl.BlockSpec((step, BLOCK, HALF), lambda i: (i, 0, 0)),
        ],
        out_specs=pl.BlockSpec((EXPERTS, step, EXP_CAP, HALF), lambda i: (0, i, 0, 0)),
        out_shape=jax.ShapeDtypeStruct((EXPERTS, Z, EXP_CAP, HALF), jnp.bfloat16),
        cost_estimate=pl.CostEstimate(flops=2 * Z * 512 * 64 * 128, bytes_accessed=3 * MIB, transcendentals=0),
    )(slots, rows)


def mix_kernel(slots_ref, gates_ref, rows_ref, out_ref):
    for z in range(slots_ref.shape[0]):
        grid = lax.broadcasted_iota(jnp.int32, (BLOCK, EXPERTS * EXP_CAP), 1).astype(jnp.float32)
        weight = jnp.zeros((BLOCK, EXPERTS * EXP_CAP), jnp.float32)
        for p in range(TOPK):
            weight = jnp.where(grid == slots_ref[z, :, p : p + 1], gates_ref[z, :, p : p + 1], weight)
        high = weight.astype(jnp.bfloat16)
        low = (weight - high.astype(jnp.float32)).astype(jnp.bfloat16)
        rows = rows_ref[:, z].reshape(EXPERTS * EXP_CAP, HALF)
        out = jnp.dot(high, rows, preferred_element_type=jnp.float32)
        out += jnp.dot(low, rows, preferred_element_type=jnp.float32)
        out_ref[z] = out.astype(jnp.bfloat16)


def mix_rows(slots, gates, rows):
    step = 8
    return pl.pallas_call(
        mix_kernel,
        grid=(Z // step,),
        in_specs=[
            pl.BlockSpec((step, BLOCK, TOPK), lambda i: (i, 0, 0)),
            pl.BlockSpec((step, BLOCK, TOPK), lambda i: (i, 0, 0)),
            pl.BlockSpec((EXPERTS, step, EXP_CAP, HALF), lambda i: (0, i, 0, 0)),
        ],
        out_specs=pl.BlockSpec((step, BLOCK, HALF), lambda i: (i, 0, 0)),
        out_shape=jax.ShapeDtypeStruct((Z, BLOCK, HALF), jnp.bfloat16),
        cost_estimate=pl.CostEstimate(flops=4 * Z * 512 * 64 * 128, bytes_accessed=3 * MIB, transcendentals=0),
    )(slots.transpose(0, 2, 1), gates.transpose(0, 2, 1), rows)


def expert_kernel(a_ref, b_ref, in_ref, down_ref, oa_ref, ob_ref, raw, normed):
    group = a_ref.shape[0]
    rows = group * EXP_CAP
    cols = EXPERTS
    total = jnp.zeros((rows, HALF), jnp.float32)
    for c in range(cols):
        a = a_ref[:, c].reshape(rows, HALF).astype(jnp.float32)
        b = b_ref[c].reshape(rows, HALF).astype(jnp.float32)
        raw[:, 2 * c * HALF : (2 * c + 1) * HALF] = a
        raw[:, (2 * c + 1) * HALF : (2 * c + 2) * HALF] = b
        total += a + b
    width = 2 * cols * HALF
    center = jnp.sum(total, axis=1, keepdims=True) / width
    spread = jnp.zeros((rows, HALF), jnp.float32)
    for c in range(2 * cols):
        off = raw[:, c * HALF : (c + 1) * HALF] - center
        spread += off * off
    scale = lax.rsqrt(jnp.sum(spread, axis=1, keepdims=True) / width + 1e-05)
    for c in range(2 * cols):
        off = raw[:, c * HALF : (c + 1) * HALF] - center
        normed[:, c * HALF : (c + 1) * HALF] = (off * scale).astype(jnp.bfloat16)
    hidden = []
    for k in range(2):
        h = jnp.dot(normed[...], in_ref[k], preferred_element_type=jnp.float32)
        hidden.append((h * (1.0 / (1.0 + jnp.exp(-h)))).astype(jnp.bfloat16))
    chunk = 512
    for j in range(width // chunk):
        cut = slice(j * chunk, (j + 1) * chunk)
        out = jnp.dot(hidden[0], down_ref[0, :, cut], preferred_element_type=jnp.float32)
        out += jnp.dot(hidden[1], down_ref[1, :, cut], preferred_element_type=jnp.float32)
        out = out.astype(jnp.bfloat16)
        for i in range(chunk // (2 * HALF)):
            c = j * (chunk // (2 * HALF)) + i
            oa_ref[:, c] = out[:, 2 * i * HALF : (2 * i + 1) * HALF].reshape(group, EXP_CAP, HALF)
            ob_ref[c] = out[:, (2 * i + 1) * HALF : (2 * i + 2) * HALF].reshape(group, EXP_CAP, HALF)


def experts(rows_a, rows_b, w_in, w_down):
    group = 4
    rows = group * EXP_CAP
    width = w_down.shape[2]
    spec_a = pl.BlockSpec((group, EXPERTS, EXP_CAP, HALF), lambda i: (i, 0, 0, 0))
    spec_b = pl.BlockSpec((EXPERTS, group, EXP_CAP, HALF), lambda i: (0, i, 0, 0))
    return pl.pallas_call(
        expert_kernel,
        grid=(Z // group,),
        in_specs=[
            spec_a,
            spec_b,
            pl.BlockSpec(w_in.shape, lambda i: (0, 0, 0)),
            pl.BlockSpec(w_down.shape, lambda i: (0, 0, 0)),
        ],
        out_specs=[spec_a, spec_b],
        out_shape=[
            jax.ShapeDtypeStruct(rows_a.shape, jnp.bfloat16),
            jax.ShapeDtypeStruct(rows_b.shape, jnp.bfloat16),
        ],
        scratch_shapes=[pltpu.VMEM((rows, width), jnp.float32), pltpu.VMEM((rows, width), jnp.bfloat16)],
        compiler_params=pltpu.CompilerParams(vmem_limit_bytes=48 * MIB),
        cost_estimate=pl.CostEstimate(flops=4 * 512 * 512 * width, bytes_accessed=16 * MIB, transcendentals=512 * 512),
    )(rows_a, rows_b, w_in, w_down)


def attend(query, k, v, tensor_place):
    block = query.shape[0]
    heads = query.shape[1] // HEAD_DIM
    total = k.shape[0]
    q = query.reshape(block, heads, HEAD_DIM)
    scores = jnp.einsum("qhd,kd->hqk", q, k, preferred_element_type=jnp.float32)
    scores = scores / math.sqrt(HEAD_DIM)
    query_pos = tensor_place * block + jnp.arange(block)
    causal = query_pos[:, None] >= jnp.arange(total)[None, :]
    scores = jnp.where(causal[None], scores, -1e30)
    top = jnp.max(scores, axis=-1, keepdims=True)
    raised = jnp.exp(scores - top)
    probs = (raised / jnp.sum(raised, axis=-1, keepdims=True)).astype(jnp.bfloat16)
    out = jnp.einsum("hqk,kd->qhd", probs, v, preferred_element_type=jnp.float32)
    return out.reshape(block, heads * HEAD_DIM)


def ranks_of(ids):
    grid = jnp.arange(EXPERTS, dtype=jnp.int32)
    picked = ids[:, :, None] == grid[None, None, :]
    chosen = jnp.any(picked, axis=1)
    rows = ids.shape[0]
    lower = (jnp.arange(rows)[:, None] > jnp.arange(rows)[None, :]).astype(jnp.bfloat16)
    rank = jnp.dot(lower, chosen.astype(jnp.bfloat16), preferred_element_type=jnp.float32).astype(jnp.int32)
    return jnp.sum(jnp.where(picked, rank[:, None, :], 0), axis=2)


def swap_columns(x):
    return lax.all_to_all(x, E, split_axis=0, concat_axis=0, tiled=True)


def per_device(query, keys, values, resid, route_ids, route_weight, w_in, w_down):
    w_in = lax.all_gather(w_in, "core", axis=0, tiled=True)
    w_down = lax.all_gather(w_down, "core", axis=0, tiled=True)
    ranks = ranks_of(route_ids)
    gates = route_weight / jnp.sum(route_weight, axis=1, keepdims=True)
    k, v, notes = gather_kv(keys, values, notes_of(route_ids, ranks, gates))
    plane_slots, plane_gates = read_notes(notes)
    attended = attend(query, k, v, lax.axis_index(T))
    state = (resid.astype(jnp.float32) + attended).astype(jnp.bfloat16)

    slot_grid = jnp.arange(EXPERTS * EXP_CAP, dtype=jnp.int32)
    slots = route_ids * EXP_CAP + ranks
    takes = (slots[:, :, None] == slot_grid[None, None, :]).astype(jnp.bfloat16)
    sent_a = jnp.einsum("tps,td->sd", takes, state[:, :HALF], preferred_element_type=jnp.float32)
    sent_a = sent_a.astype(jnp.bfloat16).reshape(EXPERTS, EXP_CAP, HALF)
    came_a = swap_columns(sent_a)
    rows_a = lax.all_gather(came_a, "z", axis=0)

    state_b, came_a = lax.optimization_barrier((state[:, HALF:], came_a))
    plane_b = lax.all_gather(state_b, "z", axis=0)
    rows_b = swap_columns(place_rows(plane_slots, plane_b))

    out_a, out_b = experts(rows_a, rows_b, w_in, w_down)

    sum_a = lax.psum_scatter(out_a, "z", scatter_dimension=0)
    part_b = mix_rows(plane_slots, plane_gates, swap_columns(out_b))
    mix_b = lax.all_to_all(part_b, "z", split_axis=0, concat_axis=0, tiled=True)
    mix_b = jnp.sum(mix_b.astype(jnp.float32), axis=0)

    back_a = swap_columns(sum_a).reshape(EXPERTS * EXP_CAP, HALF)
    outs_a = jnp.einsum("tps,sd->tpd", takes, back_a, preferred_element_type=jnp.float32)
    mix_a = jnp.sum(gates[:, :, None] * outs_a, axis=1)
    mixture = jnp.concatenate([mix_a, mix_b], axis=1)
    return (state.astype(jnp.float32) + mixture).astype(jnp.bfloat16)


def solution(mesh):
    fine = Mesh(mesh.devices.reshape(4, 4, 16, 2), ("x", "y", "z", "core"))
    placed = (
        P(T, E),
        P(T, None),
        P(T, None),
        P(T, E),
        P(T, None),
        P(T, None),
        P(E, None, T),
        P(E, T, None),
    )
    return jax.shard_map(per_device, mesh=fine, in_specs=placed, out_specs=P(T, E), check_vma=False)
```

```python
import math

import jax
import jax.numpy as jnp
from jax import lax
from jax.experimental import pallas as pl
from jax.experimental.pallas import tpu as pltpu
from jax.sharding import Mesh
from jax.sharding import PartitionSpec as P

HEADS = 32
KV_HEADS = 8
HEAD_DIM = 128
EXPERTS = 16
EXP_CAP = 32
TOPK = 4
BLOCK = 64
HALF = 128
Z = 16
MIB = 1 << 20

E = ("x", "y")
T = ("z", "core")


def swap_cores(x):
    return lax.ppermute(x, "core", [(0, 1), (1, 0)])


def gather_kv(keys, values, notes):
    group = lax.axis_index(E) // 2
    core = lax.axis_index("core")
    k = lax.dynamic_slice_in_dim(keys, group * HEAD_DIM, HEAD_DIM, 1)
    v = lax.dynamic_slice_in_dim(values, group * HEAD_DIM, HEAD_DIM, 1)
    first = core == 0
    came = swap_cores(jnp.where(first, v, k))
    kept = jnp.where(first, k, v)
    chip = jnp.concatenate([jnp.where(first, kept, came), jnp.where(first, came, kept), notes], axis=0)
    all_chips = lax.all_gather(chip, "z", axis=0)
    mine = all_chips[:, : 2 * BLOCK].reshape(-1, HEAD_DIM)
    other = swap_cores(mine)
    return jnp.where(first, mine, other), jnp.where(first, other, mine), all_chips[:, 2 * BLOCK :]


def notes_of(ids, ranks, gates):
    top = lax.reduce_precision(gates, 8, 7)
    rest = gates - top
    middle = lax.reduce_precision(rest, 8, 7)
    low = rest - middle
    parts = [ids.astype(jnp.float32), ranks.astype(jnp.float32), top, middle, low]
    rows = jnp.concatenate([p.T.reshape(2, 128) for p in parts], axis=0).astype(jnp.bfloat16)
    return jnp.pad(rows, ((0, 6), (0, 0)))


def read_notes(notes):
    rows = notes[:, :10].astype(jnp.float32).reshape(Z, 5, TOPK, BLOCK)
    return rows[:, 0] * EXP_CAP + rows[:, 1], rows[:, 2] + rows[:, 3] + rows[:, 4]


def grids_kernel(slots_ref, slots_t_ref, gates_ref, take_ref, high_ref, low_ref):
    slots = EXPERTS * EXP_CAP
    for z in range(slots_ref.shape[0]):
        grid = lax.broadcasted_iota(jnp.int32, (slots, BLOCK), 0).astype(jnp.float32)
        hit = grid == slots_t_ref[z, 0:1, :]
        for p in range(1, TOPK):
            hit = jnp.logical_or(hit, grid == slots_t_ref[z, p : p + 1, :])
        take_ref[z] = jnp.where(hit, 1.0, 0.0).astype(jnp.bfloat16)
        grid = lax.broadcasted_iota(jnp.int32, (BLOCK, slots), 1).astype(jnp.float32)
        weight = jnp.zeros((BLOCK, slots), jnp.float32)
        for p in range(TOPK):
            weight = jnp.where(grid == slots_ref[z, :, p : p + 1], gates_ref[z, :, p : p + 1], weight)
        high = weight.astype(jnp.bfloat16)
        high_ref[z] = high
        low_ref[z] = (weight - high.astype(jnp.float32)).astype(jnp.bfloat16)


def grids(slots, gates):
    step = 4
    total = EXPERTS * EXP_CAP
    return pl.pallas_call(
        grids_kernel,
        grid=(Z // step,),
        in_specs=[
            pl.BlockSpec((step, BLOCK, TOPK), lambda i: (i, 0, 0)),
            pl.BlockSpec((step, TOPK, BLOCK), lambda i: (i, 0, 0)),
            pl.BlockSpec((step, BLOCK, TOPK), lambda i: (i, 0, 0)),
        ],
        out_specs=[
            pl.BlockSpec((step, total, BLOCK), lambda i: (i, 0, 0)),
            pl.BlockSpec((step, BLOCK, total), lambda i: (i, 0, 0)),
            pl.BlockSpec((step, BLOCK, total), lambda i: (i, 0, 0)),
        ],
        out_shape=[
            jax.ShapeDtypeStruct((Z, total, BLOCK), jnp.bfloat16),
            jax.ShapeDtypeStruct((Z, BLOCK, total), jnp.bfloat16),
            jax.ShapeDtypeStruct((Z, BLOCK, total), jnp.bfloat16),
        ],
        cost_estimate=pl.CostEstimate(flops=16 * MIB, bytes_accessed=4 * MIB, transcendentals=0),
    )(slots.transpose(0, 2, 1), slots, gates.transpose(0, 2, 1))


def place_kernel(take_ref, rows_ref, out_ref):
    for z in range(take_ref.shape[0]):
        out = jnp.dot(take_ref[z], rows_ref[z], preferred_element_type=jnp.float32).astype(jnp.bfloat16)
        out_ref[:, z] = out.reshape(EXPERTS, EXP_CAP, HALF)


def place_rows(take, rows):
    step = 4
    return pl.pallas_call(
        place_kernel,
        grid=(Z // step,),
        in_specs=[
            pl.BlockSpec((step, EXPERTS * EXP_CAP, BLOCK), lambda i: (i, 0, 0)),
            pl.BlockSpec((step, BLOCK, HALF), lambda i: (i, 0, 0)),
        ],
        out_specs=pl.BlockSpec((EXPERTS, step, EXP_CAP, HALF), lambda i: (0, i, 0, 0)),
        out_shape=jax.ShapeDtypeStruct((EXPERTS, Z, EXP_CAP, HALF), jnp.bfloat16),
        cost_estimate=pl.CostEstimate(flops=2 * Z * 512 * 64 * 128, bytes_accessed=5 * MIB, transcendentals=0),
    )(take, rows)


def mix_kernel(high_ref, low_ref, rows_ref, out_ref):
    for z in range(high_ref.shape[0]):
        rows = rows_ref[:, z].reshape(EXPERTS * EXP_CAP, HALF)
        out = jnp.dot(high_ref[z], rows, preferred_element_type=jnp.float32)
        out += jnp.dot(low_ref[z], rows, preferred_element_type=jnp.float32)
        out_ref[z] = out.astype(jnp.bfloat16)


def mix_rows(high, low, rows):
    step = 4
    weights = pl.BlockSpec((step, BLOCK, EXPERTS * EXP_CAP), lambda i: (i, 0, 0))
    return pl.pallas_call(
        mix_kernel,
        grid=(Z // step,),
        in_specs=[
            weights,
            weights,
            pl.BlockSpec((EXPERTS, step, EXP_CAP, HALF), lambda i: (0, i, 0, 0)),
        ],
        out_specs=pl.BlockSpec((step, BLOCK, HALF), lambda i: (i, 0, 0)),
        out_shape=jax.ShapeDtypeStruct((Z, BLOCK, HALF), jnp.bfloat16),
        cost_estimate=pl.CostEstimate(flops=4 * Z * 512 * 64 * 128, bytes_accessed=5 * MIB, transcendentals=0),
    )(high, low, rows)


def expert_kernel(a_ref, b_ref, in_ref, down_ref, oa_ref, ob_ref, raw, normed):
    group = a_ref.shape[1]
    rows = group * EXP_CAP
    cols = EXPERTS
    width = 2 * cols * HALF
    hidden = []
    for k in range(2):
        h = jnp.dot(normed[...], in_ref[k], preferred_element_type=jnp.float32)
        hidden.append((h * (1.0 / (1.0 + jnp.exp(-h)))).astype(jnp.bfloat16))
    chunk = 512
    for j in range(width // chunk):
        cut = slice(j * chunk, (j + 1) * chunk)
        out = jnp.dot(hidden[0], down_ref[0, :, cut], preferred_element_type=jnp.float32)
        out += jnp.dot(hidden[1], down_ref[1, :, cut], preferred_element_type=jnp.float32)
        out = out.astype(jnp.bfloat16)
        for i in range(chunk // (2 * HALF)):
            c = j * (chunk // (2 * HALF)) + i
            oa_ref[c] = out[:, 2 * i * HALF : (2 * i + 1) * HALF].reshape(group, EXP_CAP, HALF)
            ob_ref[c] = out[:, (2 * i + 1) * HALF : (2 * i + 2) * HALF].reshape(group, EXP_CAP, HALF)
    total = jnp.zeros((rows, HALF), jnp.float32)
    for c in range(cols):
        a = a_ref[c].reshape(rows, HALF).astype(jnp.float32)
        b = b_ref[c].reshape(rows, HALF).astype(jnp.float32)
        raw[:, 2 * c * HALF : (2 * c + 1) * HALF] = a
        raw[:, (2 * c + 1) * HALF : (2 * c + 2) * HALF] = b
        total += a + b
    center = jnp.sum(total, axis=1, keepdims=True) / width
    spread = jnp.zeros((rows, HALF), jnp.float32)
    for c in range(2 * cols):
        off = raw[:, c * HALF : (c + 1) * HALF] - center
        spread += off * off
    scale = lax.rsqrt(jnp.sum(spread, axis=1, keepdims=True) / width + 1e-05)
    for c in range(2 * cols):
        off = raw[:, c * HALF : (c + 1) * HALF] - center
        normed[:, c * HALF : (c + 1) * HALF] = (off * scale).astype(jnp.bfloat16)


def experts(rows_a, rows_b, w_in, w_down):
    group = 4
    rows = group * EXP_CAP
    steps = Z // group
    width = w_down.shape[2]
    block = (EXPERTS, group, EXP_CAP, HALF)
    spec_in = pl.BlockSpec(block, lambda i: (0, jnp.minimum(i, steps - 1), 0, 0))
    spec_out = pl.BlockSpec(block, lambda i: (0, jnp.maximum(i - 1, 0), 0, 0))
    return pl.pallas_call(
        expert_kernel,
        grid=(steps + 1,),
        in_specs=[
            spec_in,
            spec_in,
            pl.BlockSpec(w_in.shape, lambda i: (0, 0, 0)),
            pl.BlockSpec(w_down.shape, lambda i: (0, 0, 0)),
        ],
        out_specs=[spec_out, spec_out],
        out_shape=[jax.ShapeDtypeStruct(rows_a.shape, jnp.bfloat16)] * 2,
        scratch_shapes=[pltpu.VMEM((rows, width), jnp.float32), pltpu.VMEM((rows, width), jnp.bfloat16)],
        compiler_params=pltpu.CompilerParams(vmem_limit_bytes=48 * MIB),
        cost_estimate=pl.CostEstimate(flops=4 * 512 * 512 * width, bytes_accessed=16 * MIB, transcendentals=512 * 512),
    )(rows_a, rows_b, w_in, w_down)


def attend(query, k, v, tensor_place):
    block = query.shape[0]
    heads = query.shape[1] // HEAD_DIM
    total = k.shape[0]
    q = query.reshape(block, heads, HEAD_DIM)
    scores = jnp.einsum("qhd,kd->hqk", q, k, preferred_element_type=jnp.float32)
    scores = scores / math.sqrt(HEAD_DIM)
    query_pos = tensor_place * block + jnp.arange(block)
    causal = query_pos[:, None] >= jnp.arange(total)[None, :]
    scores = jnp.where(causal[None], scores, -1e30)
    top = jnp.max(scores, axis=-1, keepdims=True)
    raised = jnp.exp(scores - top)
    probs = (raised / jnp.sum(raised, axis=-1, keepdims=True)).astype(jnp.bfloat16)
    out = jnp.einsum("hqk,kd->qhd", probs, v, preferred_element_type=jnp.float32)
    return out.reshape(block, heads * HEAD_DIM)


def ranks_of(ids):
    grid = jnp.arange(EXPERTS, dtype=jnp.int32)
    picked = ids[:, :, None] == grid[None, None, :]
    chosen = jnp.any(picked, axis=1)
    rows = ids.shape[0]
    lower = (jnp.arange(rows)[:, None] > jnp.arange(rows)[None, :]).astype(jnp.bfloat16)
    rank = jnp.dot(lower, chosen.astype(jnp.bfloat16), preferred_element_type=jnp.float32).astype(jnp.int32)
    return jnp.sum(jnp.where(picked, rank[:, None, :], 0), axis=2)


def swap_columns(x):
    return lax.all_to_all(x, E, split_axis=0, concat_axis=0, tiled=True)


def swap_chips(x):
    return lax.all_to_all(x, "z", split_axis=0, concat_axis=0, tiled=True)


def per_device(query, keys, values, resid, route_ids, route_weight, w_in, w_down):
    w_in = lax.all_gather(w_in, "core", axis=0, tiled=True)
    w_down = lax.all_gather(w_down, "core", axis=0, tiled=True)
    ranks = ranks_of(route_ids)
    gates = route_weight / jnp.sum(route_weight, axis=1, keepdims=True)
    k, v, notes = gather_kv(keys, values, notes_of(route_ids, ranks, gates))
    plane_slots, plane_gates = read_notes(notes)
    attended = attend(query, k, v, lax.axis_index(T))
    state = (resid.astype(jnp.float32) + attended).astype(jnp.bfloat16)

    take, high, low = grids(plane_slots, plane_gates)
    rows = []
    for cut in (state[:, :HALF], state[:, HALF:]):
        plane = swap_chips(jnp.broadcast_to(cut[None], (Z, BLOCK, HALF)))
        rows.append(swap_columns(place_rows(take, plane)))
    mixes = []
    for part in experts(*rows, w_in, w_down):
        mix = swap_chips(mix_rows(high, low, swap_columns(part)))
        mixes.append(jnp.sum(mix.astype(jnp.float32), axis=0))
    mixture = jnp.concatenate(mixes, axis=1)
    return (state.astype(jnp.float32) + mixture).astype(jnp.bfloat16)


def solution(mesh):
    fine = Mesh(mesh.devices.reshape(4, 4, 16, 2), ("x", "y", "z", "core"))
    placed = (
        P(T, E),
        P(T, None),
        P(T, None),
        P(T, E),
        P(T, None),
        P(T, None),
        P(E, None, T),
        P(E, T, None),
    )
    return jax.shard_map(per_device, mesh=fine, in_specs=placed, out_specs=P(T, E), check_vma=False)
```

```python
import math

import jax
import jax.numpy as jnp
from jax import lax
from jax.experimental import pallas as pl
from jax.experimental.pallas import tpu as pltpu
from jax.sharding import Mesh
from jax.sharding import PartitionSpec as P

HEADS = 32
KV_HEADS = 8
HEAD_DIM = 128
EXPERTS = 16
EXP_CAP = 32
TOPK = 4
BLOCK = 64
WIDTH = 256
Z = 16
PARTS = 2
MIB = 1 << 20

E = ("x", "y")
T = ("z", "core")


def swap_cores(x):
    return lax.ppermute(x, "core", [(0, 1), (1, 0)])


def gather_kv(keys, values, notes):
    group = lax.axis_index(E) // 2
    core = lax.axis_index("core")
    k = lax.dynamic_slice_in_dim(keys, group * HEAD_DIM, HEAD_DIM, 1)
    v = lax.dynamic_slice_in_dim(values, group * HEAD_DIM, HEAD_DIM, 1)
    first = core == 0
    came = swap_cores(jnp.where(first, v, k))
    kept = jnp.where(first, k, v)
    chip = jnp.concatenate([jnp.where(first, kept, came), jnp.where(first, came, kept), notes], axis=0)
    all_chips = lax.all_gather(chip, "z", axis=0)
    mine = all_chips[:, : 2 * BLOCK].reshape(-1, HEAD_DIM)
    other = swap_cores(mine)
    return jnp.where(first, mine, other), jnp.where(first, other, mine), all_chips[:, 2 * BLOCK :]


def notes_of(ids, ranks, gates):
    top = lax.reduce_precision(gates, 8, 7)
    rest = gates - top
    middle = lax.reduce_precision(rest, 8, 7)
    low = rest - middle
    parts = [ids.astype(jnp.float32), ranks.astype(jnp.float32), top, middle, low]
    rows = jnp.concatenate([p.T.reshape(2, 128) for p in parts], axis=0).astype(jnp.bfloat16)
    return jnp.pad(rows, ((0, 6), (0, 0)))


def read_notes(notes):
    rows = notes[:, :10].astype(jnp.float32).reshape(Z, 5, TOPK, BLOCK)
    return rows[:, 0] * EXP_CAP + rows[:, 1], rows[:, 2] + rows[:, 3] + rows[:, 4]


def place_kernel(slots_ref, rows_ref, out_ref):
    for z in range(slots_ref.shape[0]):
        grid = lax.broadcasted_iota(jnp.int32, (EXPERTS * EXP_CAP, BLOCK), 0).astype(jnp.float32)
        hit = grid == slots_ref[z, 0:1, :]
        for p in range(1, TOPK):
            hit = jnp.logical_or(hit, grid == slots_ref[z, p : p + 1, :])
        take = jnp.where(hit, 1.0, 0.0).astype(jnp.bfloat16)
        out = jnp.dot(take, rows_ref[z], preferred_element_type=jnp.float32).astype(jnp.bfloat16)
        out_ref[:, z] = out.reshape(EXPERTS, EXP_CAP, WIDTH)


def place_rows(slots, rows, part):
    step = 4
    count = Z // PARTS
    first = part * count // step
    return pl.pallas_call(
        place_kernel,
        grid=(count // step,),
        in_specs=[
            pl.BlockSpec((step, TOPK, BLOCK), lambda i: (first + i, 0, 0)),
            pl.BlockSpec((step, BLOCK, WIDTH), lambda i: (first + i, 0, 0)),
        ],
        out_specs=pl.BlockSpec((EXPERTS, step, EXP_CAP, WIDTH), lambda i: (0, i, 0, 0)),
        out_shape=jax.ShapeDtypeStruct((EXPERTS, count, EXP_CAP, WIDTH), jnp.bfloat16),
        compiler_params=pltpu.CompilerParams(vmem_limit_bytes=32 * MIB),
        cost_estimate=pl.CostEstimate(flops=2 * Z * 512 * 64 * 128, bytes_accessed=3 * MIB, transcendentals=0),
    )(slots, rows)


def mix_kernel(slots_ref, gates_ref, rows_ref, out_ref):
    for z in range(slots_ref.shape[0]):
        grid = lax.broadcasted_iota(jnp.int32, (BLOCK, EXPERTS * EXP_CAP), 1).astype(jnp.float32)
        weight = jnp.zeros((BLOCK, EXPERTS * EXP_CAP), jnp.float32)
        for p in range(TOPK):
            weight = jnp.where(grid == slots_ref[z, :, p : p + 1], gates_ref[z, :, p : p + 1], weight)
        high = weight.astype(jnp.bfloat16)
        low = (weight - high.astype(jnp.float32)).astype(jnp.bfloat16)
        rows = rows_ref[:, z].reshape(EXPERTS * EXP_CAP, WIDTH)
        out = jnp.dot(high, rows, preferred_element_type=jnp.float32)
        out += jnp.dot(low, rows, preferred_element_type=jnp.float32)
        out_ref[z] = out.astype(jnp.bfloat16)


def mix_rows(slots, gates, rows, part):
    step = 4
    count = Z // PARTS
    first = part * count // step
    return pl.pallas_call(
        mix_kernel,
        grid=(count // step,),
        in_specs=[
            pl.BlockSpec((step, BLOCK, TOPK), lambda i: (first + i, 0, 0)),
            pl.BlockSpec((step, BLOCK, TOPK), lambda i: (first + i, 0, 0)),
            pl.BlockSpec((EXPERTS, step, EXP_CAP, WIDTH), lambda i: (0, i, 0, 0)),
        ],
        out_specs=pl.BlockSpec((step, BLOCK, WIDTH), lambda i: (i, 0, 0)),
        out_shape=jax.ShapeDtypeStruct((count, BLOCK, WIDTH), jnp.bfloat16),
        compiler_params=pltpu.CompilerParams(vmem_limit_bytes=32 * MIB),
        cost_estimate=pl.CostEstimate(flops=4 * Z * 512 * 64 * 128, bytes_accessed=3 * MIB, transcendentals=0),
    )(slots, gates, rows)


def expert_kernel(rows_ref, in_ref, down_ref, out_ref, raw, normed):
    group = rows_ref.shape[1]
    rows = group * EXP_CAP
    width = EXPERTS * WIDTH
    total = jnp.zeros((rows, WIDTH), jnp.float32)
    for c in range(EXPERTS):
        part = rows_ref[c].reshape(rows, WIDTH).astype(jnp.float32)
        raw[:, c * WIDTH : (c + 1) * WIDTH] = part
        total += part
    center = jnp.sum(total, axis=1, keepdims=True) / width
    spread = jnp.zeros((rows, WIDTH), jnp.float32)
    for c in range(EXPERTS):
        off = raw[:, c * WIDTH : (c + 1) * WIDTH] - center
        spread += off * off
    scale = lax.rsqrt(jnp.sum(spread, axis=1, keepdims=True) / width + 1e-05)
    for c in range(EXPERTS):
        off = raw[:, c * WIDTH : (c + 1) * WIDTH] - center
        normed[:, c * WIDTH : (c + 1) * WIDTH] = (off * scale).astype(jnp.bfloat16)
    hidden = []
    for k in range(2):
        h = jnp.dot(normed[...], in_ref[k], preferred_element_type=jnp.float32)
        hidden.append((h * (1.0 / (1.0 + jnp.exp(-h)))).astype(jnp.bfloat16))
    for c in range(EXPERTS):
        cut = slice(c * WIDTH, (c + 1) * WIDTH)
        out = jnp.dot(hidden[0], down_ref[0, :, cut], preferred_element_type=jnp.float32)
        out += jnp.dot(hidden[1], down_ref[1, :, cut], preferred_element_type=jnp.float32)
        out_ref[c] = out.astype(jnp.bfloat16).reshape(group, EXP_CAP, WIDTH)


def experts(rows, w_in, w_down):
    group = 4
    width = w_down.shape[2]
    count = rows.shape[1]
    spec = pl.BlockSpec((EXPERTS, group, EXP_CAP, WIDTH), lambda i: (0, i, 0, 0))
    return pl.pallas_call(
        expert_kernel,
        grid=(count // group,),
        in_specs=[
            spec,
            pl.BlockSpec(w_in.shape, lambda i: (0, 0, 0)),
            pl.BlockSpec(w_down.shape, lambda i: (0, 0, 0)),
        ],
        out_specs=spec,
        out_shape=jax.ShapeDtypeStruct(rows.shape, jnp.bfloat16),
        scratch_shapes=[
            pltpu.VMEM((group * EXP_CAP, width), jnp.float32),
            pltpu.VMEM((group * EXP_CAP, width), jnp.bfloat16),
        ],
        compiler_params=pltpu.CompilerParams(vmem_limit_bytes=48 * MIB),
        cost_estimate=pl.CostEstimate(flops=2 * 512 * 512 * width, bytes_accessed=12 * MIB, transcendentals=256 * 512),
    )(rows, w_in, w_down)


def attend(query, k, v, tensor_place):
    block = query.shape[0]
    heads = query.shape[1] // HEAD_DIM
    total = k.shape[0]
    q = query.reshape(block, heads, HEAD_DIM)
    scores = jnp.einsum("qhd,kd->hqk", q, k, preferred_element_type=jnp.float32)
    scores = scores / math.sqrt(HEAD_DIM)
    query_pos = tensor_place * block + jnp.arange(block)
    causal = query_pos[:, None] >= jnp.arange(total)[None, :]
    scores = jnp.where(causal[None], scores, -1e30)
    top = jnp.max(scores, axis=-1, keepdims=True)
    raised = jnp.exp(scores - top)
    probs = (raised / jnp.sum(raised, axis=-1, keepdims=True)).astype(jnp.bfloat16)
    out = jnp.einsum("hqk,kd->qhd", probs, v, preferred_element_type=jnp.float32)
    return out.reshape(block, heads * HEAD_DIM)


def ranks_of(ids):
    grid = jnp.arange(EXPERTS, dtype=jnp.int32)
    picked = ids[:, :, None] == grid[None, None, :]
    chosen = jnp.any(picked, axis=1)
    rows = ids.shape[0]
    lower = (jnp.arange(rows)[:, None] > jnp.arange(rows)[None, :]).astype(jnp.bfloat16)
    rank = jnp.dot(lower, chosen.astype(jnp.bfloat16), preferred_element_type=jnp.float32).astype(jnp.int32)
    return jnp.sum(jnp.where(picked, rank[:, None, :], 0), axis=2)


def swap_columns(x):
    return lax.all_to_all(x, E, split_axis=0, concat_axis=0, tiled=True)


def swap_chips(x):
    return lax.all_to_all(x, "z", split_axis=0, concat_axis=0, tiled=True)


def per_device(query, keys, values, resid, route_ids, route_weight, w_in, w_down):
    w_in = lax.all_gather(w_in, "core", axis=0, tiled=True)
    w_down = lax.all_gather(w_down, "core", axis=0, tiled=True)
    ranks = ranks_of(route_ids)
    gates = route_weight / jnp.sum(route_weight, axis=1, keepdims=True)
    k, v, notes = gather_kv(keys, values, notes_of(route_ids, ranks, gates))
    plane_slots, plane_gates = read_notes(notes)
    attended = attend(query, k, v, lax.axis_index(T))
    state = (resid.astype(jnp.float32) + attended).astype(jnp.bfloat16)

    slots_t, gates_t = plane_slots.transpose(0, 2, 1), plane_gates.transpose(0, 2, 1)
    plane = lax.all_gather(state, "z", axis=0)
    rows = [swap_columns(place_rows(plane_slots, plane, part)) for part in range(PARTS)]
    outs = [experts(part, w_in, w_down) for part in rows]
    outs[0], rows[1] = lax.optimization_barrier((outs[0], rows[1]))
    mixes = [mix_rows(slots_t, gates_t, swap_columns(out), part) for part, out in enumerate(outs)]
    mix = swap_chips(jnp.concatenate(mixes, axis=0))
    mixture = jnp.sum(mix.astype(jnp.float32), axis=0)
    return (state.astype(jnp.float32) + mixture).astype(jnp.bfloat16)


def solution(mesh):
    fine = Mesh(mesh.devices.reshape(4, 4, 16, 2), ("x", "y", "z", "core"))
    placed = (
        P(T, E),
        P(T, None),
        P(T, None),
        P(T, E),
        P(T, None),
        P(T, None),
        P(E, None, T),
        P(E, T, None),
    )
    return jax.shard_map(per_device, mesh=fine, in_specs=placed, out_specs=P(T, E), check_vma=False)
```

```python
import math

import jax
import jax.numpy as jnp
from jax import lax
from jax.experimental import pallas as pl
from jax.experimental.pallas import tpu as pltpu
from jax.sharding import Mesh
from jax.sharding import PartitionSpec as P

HEADS = 32
KV_HEADS = 8
HEAD_DIM = 128
EXPERTS = 16
EXP_CAP = 32
TOPK = 4
BLOCK = 64
WIDTH = 256
Z = 16
PARTS = 2
MIB = 1 << 20

E = ("x", "y")
T = ("z", "core")


def swap_cores(x):
    return lax.ppermute(x, "core", [(0, 1), (1, 0)])


def swap_chips(x):
    return lax.all_to_all(x, "z", split_axis=0, concat_axis=0, tiled=True)


def gather_chips(x):
    return swap_chips(jnp.broadcast_to(x[None], (Z,) + x.shape))


def gather_kv(keys, values, notes):
    first = lax.axis_index(E) // 2 * HEAD_DIM
    k = lax.dynamic_slice_in_dim(keys, first, HEAD_DIM, 1)
    v = lax.dynamic_slice_in_dim(values, first, HEAD_DIM, 1)
    sent = jnp.concatenate([jnp.concatenate([k, v], axis=1), notes], axis=0)
    came = gather_chips(sent)
    mine = came[:, :BLOCK]
    both = jnp.stack([mine, swap_cores(mine)])
    return both[..., :HEAD_DIM], both[..., HEAD_DIM:], came[:, BLOCK:]


def notes_of(ids, ranks, gates):
    top = lax.reduce_precision(gates, 8, 7)
    rest = gates - top
    middle = lax.reduce_precision(rest, 8, 7)
    low = rest - middle
    parts = [ids.astype(jnp.float32), ranks.astype(jnp.float32), top, middle, low]
    rows = jnp.concatenate([p.T.reshape(1, TOPK * BLOCK) for p in parts], axis=0).astype(jnp.bfloat16)
    return jnp.pad(rows, ((0, 11), (0, 0)))


def read_notes(notes):
    rows = notes[:, :5].astype(jnp.float32).reshape(Z, 5, TOPK, BLOCK)
    return rows[:, 0] * EXP_CAP + rows[:, 1], rows[:, 2] + rows[:, 3] + rows[:, 4]


def in_hbm(x):
    return pltpu.with_memory_space_constraint(x, pltpu.MemorySpace.HBM)


def place_kernel(slots_ref, rows_ref, out_ref):
    for z in range(slots_ref.shape[0]):
        grid = lax.broadcasted_iota(jnp.int32, (EXPERTS * EXP_CAP, BLOCK), 0).astype(jnp.float32)
        hit = grid == slots_ref[z, 0:1, :]
        for p in range(1, TOPK):
            hit = jnp.logical_or(hit, grid == slots_ref[z, p : p + 1, :])
        take = jnp.where(hit, 1.0, 0.0).astype(jnp.bfloat16)
        out = jnp.dot(take, rows_ref[z], preferred_element_type=jnp.float32).astype(jnp.bfloat16)
        out_ref[:, z] = out.reshape(EXPERTS, EXP_CAP, WIDTH)


def place_rows(slots, rows, part):
    step = 4
    count = Z // PARTS
    first = part * count // step
    return pl.pallas_call(
        place_kernel,
        grid=(count // step,),
        in_specs=[
            pl.BlockSpec((step, TOPK, BLOCK), lambda i: (first + i, 0, 0)),
            pl.BlockSpec((step, BLOCK, WIDTH), lambda i: (first + i, 0, 0)),
        ],
        out_specs=pl.BlockSpec((EXPERTS, step, EXP_CAP, WIDTH), lambda i: (0, i, 0, 0)),
        out_shape=pltpu.MemorySpace.HBM((EXPERTS, count, EXP_CAP, WIDTH), jnp.bfloat16),
        compiler_params=pltpu.CompilerParams(vmem_limit_bytes=63 * MIB),
        cost_estimate=pl.CostEstimate(flops=2 * Z * 512 * 64 * 128, bytes_accessed=3 * MIB, transcendentals=0),
    )(slots, in_hbm(rows))


def mix_kernel(slots_ref, gates_ref, rows_ref, out_ref):
    for z in range(slots_ref.shape[0]):
        grid = lax.broadcasted_iota(jnp.int32, (BLOCK, EXPERTS * EXP_CAP), 1).astype(jnp.float32)
        weight = jnp.zeros((BLOCK, EXPERTS * EXP_CAP), jnp.float32)
        for p in range(TOPK):
            weight = jnp.where(grid == slots_ref[z, :, p : p + 1], gates_ref[z, :, p : p + 1], weight)
        high = weight.astype(jnp.bfloat16)
        low = (weight - high.astype(jnp.float32)).astype(jnp.bfloat16)
        rows = rows_ref[:, z].reshape(EXPERTS * EXP_CAP, WIDTH)
        out = jnp.dot(high, rows, preferred_element_type=jnp.float32)
        out += jnp.dot(low, rows, preferred_element_type=jnp.float32)
        out_ref[z] = out.astype(jnp.bfloat16)


def mix_rows(slots, gates, rows, part):
    step = 4
    count = Z // PARTS
    first = part * count // step
    return pl.pallas_call(
        mix_kernel,
        grid=(count // step,),
        in_specs=[
            pl.BlockSpec((step, BLOCK, TOPK), lambda i: (first + i, 0, 0)),
            pl.BlockSpec((step, BLOCK, TOPK), lambda i: (first + i, 0, 0)),
            pl.BlockSpec((EXPERTS, step, EXP_CAP, WIDTH), lambda i: (0, i, 0, 0)),
        ],
        out_specs=pl.BlockSpec((step, BLOCK, WIDTH), lambda i: (i, 0, 0)),
        out_shape=pltpu.MemorySpace.HBM((count, BLOCK, WIDTH), jnp.bfloat16),
        compiler_params=pltpu.CompilerParams(vmem_limit_bytes=63 * MIB),
        cost_estimate=pl.CostEstimate(flops=4 * Z * 512 * 64 * 128, bytes_accessed=3 * MIB, transcendentals=0),
    )(slots, gates, in_hbm(rows))


def expert_kernel(rows_ref, in_ref, down_ref, out_ref, raw, normed):
    group = rows_ref.shape[1]
    rows = group * EXP_CAP
    width = EXPERTS * WIDTH
    total = jnp.zeros((rows, WIDTH), jnp.float32)
    for c in range(EXPERTS):
        part = rows_ref[c].reshape(rows, WIDTH).astype(jnp.float32)
        raw[:, c * WIDTH : (c + 1) * WIDTH] = part
        total += part
    center = jnp.sum(total, axis=1, keepdims=True) / width
    spread = jnp.zeros((rows, WIDTH), jnp.float32)
    for c in range(EXPERTS):
        off = raw[:, c * WIDTH : (c + 1) * WIDTH] - center
        spread += off * off
    scale = lax.rsqrt(jnp.sum(spread, axis=1, keepdims=True) / width + 1e-05)
    for c in range(EXPERTS):
        off = raw[:, c * WIDTH : (c + 1) * WIDTH] - center
        normed[:, c * WIDTH : (c + 1) * WIDTH] = (off * scale).astype(jnp.bfloat16)
    hidden = []
    for k in range(2):
        h = jnp.dot(normed[...], in_ref[k], preferred_element_type=jnp.float32)
        hidden.append((h * (1.0 / (1.0 + jnp.exp(-h)))).astype(jnp.bfloat16))
    for c in range(EXPERTS):
        cut = slice(c * WIDTH, (c + 1) * WIDTH)
        out = jnp.dot(hidden[0], down_ref[0, :, cut], preferred_element_type=jnp.float32)
        out += jnp.dot(hidden[1], down_ref[1, :, cut], preferred_element_type=jnp.float32)
        out_ref[c] = out.astype(jnp.bfloat16).reshape(group, EXP_CAP, WIDTH)


def experts(rows, w_in, w_down):
    group = 4
    width = w_down.shape[2]
    count = rows.shape[1]
    spec = pl.BlockSpec((EXPERTS, group, EXP_CAP, WIDTH), lambda i: (0, i, 0, 0))
    return pl.pallas_call(
        expert_kernel,
        grid=(count // group,),
        in_specs=[
            spec,
            pl.BlockSpec(w_in.shape, lambda i: (0, 0, 0), pipeline_mode=pl.Buffered(1)),
            pl.BlockSpec(w_down.shape, lambda i: (0, 0, 0), pipeline_mode=pl.Buffered(1)),
        ],
        out_specs=spec,
        out_shape=pltpu.MemorySpace.HBM(rows.shape, jnp.bfloat16),
        scratch_shapes=[
            pltpu.VMEM((group * EXP_CAP, width), jnp.float32),
            pltpu.VMEM((group * EXP_CAP, width), jnp.bfloat16),
        ],
        compiler_params=pltpu.CompilerParams(vmem_limit_bytes=63 * MIB),
        cost_estimate=pl.CostEstimate(flops=2 * 512 * 512 * width, bytes_accessed=12 * MIB, transcendentals=256 * 512),
    )(in_hbm(rows), in_hbm(w_in), in_hbm(w_down))


def attend(query, k, v):
    heads = query.shape[1] // HEAD_DIM
    chip, core = lax.axis_index("z"), lax.axis_index("core")
    q = query.reshape(BLOCK, heads, HEAD_DIM)
    k = k.reshape(-1, HEAD_DIM)
    v = v.reshape(-1, HEAD_DIM)
    scores = jnp.einsum("qhd,kd->hqk", q, k, preferred_element_type=jnp.float32)
    scores = scores / math.sqrt(HEAD_DIM)
    place = jnp.arange(k.shape[0])
    key_core = jnp.where(place < Z * BLOCK, core, 1 - core)
    key_pos = (place // BLOCK % Z * 2 + key_core) * BLOCK + place % BLOCK
    query_pos = (chip * 2 + core) * BLOCK + jnp.arange(BLOCK)
    causal = query_pos[:, None] >= key_pos[None, :]
    scores = jnp.where(causal[None], scores, -1e30)
    top = jnp.max(scores, axis=-1, keepdims=True)
    raised = jnp.exp(scores - top)
    probs = (raised / jnp.sum(raised, axis=-1, keepdims=True)).astype(jnp.bfloat16)
    out = jnp.einsum("hqk,kd->qhd", probs, v, preferred_element_type=jnp.float32)
    return out.reshape(BLOCK, heads * HEAD_DIM)


def ranks_of(ids):
    grid = jnp.arange(EXPERTS, dtype=jnp.int32)
    picked = ids[:, :, None] == grid[None, None, :]
    chosen = jnp.any(picked, axis=1)
    rows = ids.shape[0]
    lower = (jnp.arange(rows)[:, None] > jnp.arange(rows)[None, :]).astype(jnp.bfloat16)
    rank = jnp.dot(lower, chosen.astype(jnp.bfloat16), preferred_element_type=jnp.float32).astype(jnp.int32)
    return jnp.sum(jnp.where(picked, rank[:, None, :], 0), axis=2)


def swap_columns(x):
    return lax.all_to_all(x, E, split_axis=0, concat_axis=0, tiled=True)


def per_device(query, keys, values, resid, route_ids, route_weight, w_in, w_down):
    w_in = lax.all_gather(w_in, "core", axis=0, tiled=True)
    w_down = lax.all_gather(w_down, "core", axis=0, tiled=True)
    ranks = ranks_of(route_ids)
    gates = route_weight / jnp.sum(route_weight, axis=1, keepdims=True)
    k, v, notes = gather_kv(keys, values, notes_of(route_ids, ranks, gates))
    plane_slots, plane_gates = read_notes(notes)
    attended = attend(query, k, v)
    state = (resid.astype(jnp.float32) + attended).astype(jnp.bfloat16)

    slots_t, gates_t = plane_slots.transpose(0, 2, 1), plane_gates.transpose(0, 2, 1)
    plane = gather_chips(state)
    rows = [swap_columns(place_rows(plane_slots, plane, part)) for part in range(PARTS)]
    outs = [experts(part, w_in, w_down) for part in rows]
    outs[0], rows[1] = lax.optimization_barrier((outs[0], rows[1]))
    mixes = [mix_rows(slots_t, gates_t, swap_columns(out), part) for part, out in enumerate(outs)]
    mix = swap_chips(jnp.concatenate(mixes, axis=0))
    mixture = jnp.sum(mix.astype(jnp.float32), axis=0)
    return (state.astype(jnp.float32) + mixture).astype(jnp.bfloat16)


def solution(mesh):
    fine = Mesh(mesh.devices.reshape(4, 4, 16, 2), ("x", "y", "z", "core"))
    placed = (
        P(T, E),
        P(T, None),
        P(T, None),
        P(T, E),
        P(T, None),
        P(T, None),
        P(E, None, T),
        P(E, T, None),
    )
    return jax.shard_map(per_device, mesh=fine, in_specs=placed, out_specs=P(T, E), check_vma=False)
```

```python
import math

import jax
import jax.numpy as jnp
from jax import lax
from jax.experimental import pallas as pl
from jax.experimental.pallas import tpu as pltpu
from jax.sharding import Mesh
from jax.sharding import PartitionSpec as P

HEADS = 32
KV_HEADS = 8
HEAD_DIM = 128
EXPERTS = 16
EXP_CAP = 32
TOPK = 4
BLOCK = 64
WIDTH = 256
Z = 16
PARTS = 2
MIB = 1 << 20

E = ("x", "y")
T = ("z", "core")


def swap_cores(x):
    return lax.ppermute(x, "core", [(0, 1), (1, 0)])


def swap_chips(x):
    return lax.all_to_all(x, "z", split_axis=0, concat_axis=0, tiled=True)


def gather_kv(keys, values):
    first = lax.axis_index(E) // 2 * HEAD_DIM
    k = lax.dynamic_slice_in_dim(keys, first, HEAD_DIM, 1)
    v = lax.dynamic_slice_in_dim(values, first, HEAD_DIM, 1)
    mine = lax.all_gather(jnp.concatenate([k, v], axis=1), "z", axis=0)
    both = jnp.stack([mine, swap_cores(mine)])
    return both[..., :HEAD_DIM], both[..., HEAD_DIM:]


def notes_of(ids, ranks, gates):
    top = lax.reduce_precision(gates, 8, 7)
    rest = gates - top
    middle = lax.reduce_precision(rest, 8, 7)
    low = rest - middle
    parts = [ids.astype(jnp.float32), ranks.astype(jnp.float32), top, middle, low]
    rows = jnp.concatenate([p.T.reshape(1, TOPK * BLOCK) for p in parts], axis=0).astype(jnp.bfloat16)
    return jnp.pad(rows, ((0, 11), (0, 0)))


def read_notes(notes):
    rows = notes[:, :5].astype(jnp.float32).reshape(Z, 5, TOPK, BLOCK)
    return rows[:, 0] * EXP_CAP + rows[:, 1], rows[:, 2] + rows[:, 3] + rows[:, 4]


def in_hbm(x):
    return pltpu.with_memory_space_constraint(x, pltpu.MemorySpace.HBM)


def place_kernel(slots_ref, rows_ref, out_ref):
    for z in range(slots_ref.shape[0]):
        grid = lax.broadcasted_iota(jnp.int32, (EXPERTS * EXP_CAP, BLOCK), 0).astype(jnp.float32)
        hit = grid == slots_ref[z, 0:1, :]
        for p in range(1, TOPK):
            hit = jnp.logical_or(hit, grid == slots_ref[z, p : p + 1, :])
        take = jnp.where(hit, 1.0, 0.0).astype(jnp.bfloat16)
        out = jnp.dot(take, rows_ref[z], preferred_element_type=jnp.float32).astype(jnp.bfloat16)
        out_ref[:, z] = out.reshape(EXPERTS, EXP_CAP, WIDTH)


def place_rows(slots, rows, part):
    step = 4
    count = Z // PARTS
    first = part * count // step
    return pl.pallas_call(
        place_kernel,
        grid=(count // step,),
        in_specs=[
            pl.BlockSpec((step, TOPK, BLOCK), lambda i: (first + i, 0, 0)),
            pl.BlockSpec((step, BLOCK, WIDTH), lambda i: (first + i, 0, 0)),
        ],
        out_specs=pl.BlockSpec((EXPERTS, step, EXP_CAP, WIDTH), lambda i: (0, i, 0, 0)),
        out_shape=pltpu.MemorySpace.HBM((EXPERTS, count, EXP_CAP, WIDTH), jnp.bfloat16),
        compiler_params=pltpu.CompilerParams(vmem_limit_bytes=63 * MIB),
        cost_estimate=pl.CostEstimate(flops=2 * Z * 512 * 64 * 128, bytes_accessed=3 * MIB, transcendentals=0),
    )(slots, in_hbm(rows))


def mix_kernel(slots_ref, gates_ref, rows_ref, out_ref):
    for z in range(slots_ref.shape[0]):
        grid = lax.broadcasted_iota(jnp.int32, (BLOCK, EXPERTS * EXP_CAP), 1).astype(jnp.float32)
        weight = jnp.zeros((BLOCK, EXPERTS * EXP_CAP), jnp.float32)
        for p in range(TOPK):
            weight = jnp.where(grid == slots_ref[z, :, p : p + 1], gates_ref[z, :, p : p + 1], weight)
        high = weight.astype(jnp.bfloat16)
        low = (weight - high.astype(jnp.float32)).astype(jnp.bfloat16)
        rows = rows_ref[:, z].reshape(EXPERTS * EXP_CAP, WIDTH)
        out = jnp.dot(high, rows, preferred_element_type=jnp.float32)
        out += jnp.dot(low, rows, preferred_element_type=jnp.float32)
        out_ref[z] = out.astype(jnp.bfloat16)


def mix_rows(slots, gates, rows, part):
    step = 4
    count = Z // PARTS
    first = part * count // step
    return pl.pallas_call(
        mix_kernel,
        grid=(count // step,),
        in_specs=[
            pl.BlockSpec((step, BLOCK, TOPK), lambda i: (first + i, 0, 0)),
            pl.BlockSpec((step, BLOCK, TOPK), lambda i: (first + i, 0, 0)),
            pl.BlockSpec((EXPERTS, step, EXP_CAP, WIDTH), lambda i: (0, i, 0, 0)),
        ],
        out_specs=pl.BlockSpec((step, BLOCK, WIDTH), lambda i: (i, 0, 0)),
        out_shape=pltpu.MemorySpace.HBM((count, BLOCK, WIDTH), jnp.bfloat16),
        compiler_params=pltpu.CompilerParams(vmem_limit_bytes=63 * MIB),
        cost_estimate=pl.CostEstimate(flops=4 * Z * 512 * 64 * 128, bytes_accessed=3 * MIB, transcendentals=0),
    )(slots, gates, in_hbm(rows))


def expert_kernel(rows_ref, in_ref, down_ref, out_ref, raw, normed):
    group = rows_ref.shape[1]
    rows = group * EXP_CAP
    width = EXPERTS * WIDTH
    total = jnp.zeros((rows, WIDTH), jnp.float32)
    for c in range(EXPERTS):
        part = rows_ref[c].reshape(rows, WIDTH).astype(jnp.float32)
        raw[:, c * WIDTH : (c + 1) * WIDTH] = part
        total += part
    center = jnp.sum(total, axis=1, keepdims=True) / width
    spread = jnp.zeros((rows, WIDTH), jnp.float32)
    for c in range(EXPERTS):
        off = raw[:, c * WIDTH : (c + 1) * WIDTH] - center
        spread += off * off
    scale = lax.rsqrt(jnp.sum(spread, axis=1, keepdims=True) / width + 1e-05)
    for c in range(EXPERTS):
        off = raw[:, c * WIDTH : (c + 1) * WIDTH] - center
        normed[:, c * WIDTH : (c + 1) * WIDTH] = (off * scale).astype(jnp.bfloat16)
    hidden = []
    for k in range(2):
        h = jnp.dot(normed[...], in_ref[k], preferred_element_type=jnp.float32)
        hidden.append((h * (1.0 / (1.0 + jnp.exp(-h)))).astype(jnp.bfloat16))
    for c in range(EXPERTS):
        cut = slice(c * WIDTH, (c + 1) * WIDTH)
        out = jnp.dot(hidden[0], down_ref[0, :, cut], preferred_element_type=jnp.float32)
        out += jnp.dot(hidden[1], down_ref[1, :, cut], preferred_element_type=jnp.float32)
        out_ref[c] = out.astype(jnp.bfloat16).reshape(group, EXP_CAP, WIDTH)


def experts(rows, w_in, w_down):
    group = 4
    width = w_down.shape[2]
    count = rows.shape[1]
    spec = pl.BlockSpec((EXPERTS, group, EXP_CAP, WIDTH), lambda i: (0, i, 0, 0))
    return pl.pallas_call(
        expert_kernel,
        grid=(count // group,),
        in_specs=[
            spec,
            pl.BlockSpec(w_in.shape, lambda i: (0, 0, 0), pipeline_mode=pl.Buffered(1)),
            pl.BlockSpec(w_down.shape, lambda i: (0, 0, 0), pipeline_mode=pl.Buffered(1)),
        ],
        out_specs=spec,
        out_shape=pltpu.MemorySpace.HBM(rows.shape, jnp.bfloat16),
        scratch_shapes=[
            pltpu.VMEM((group * EXP_CAP, width), jnp.float32),
            pltpu.VMEM((group * EXP_CAP, width), jnp.bfloat16),
        ],
        compiler_params=pltpu.CompilerParams(vmem_limit_bytes=63 * MIB),
        cost_estimate=pl.CostEstimate(flops=2 * 512 * 512 * width, bytes_accessed=12 * MIB, transcendentals=256 * 512),
    )(in_hbm(rows), in_hbm(w_in), in_hbm(w_down))


def attend(query, k, v):
    heads = query.shape[1] // HEAD_DIM
    chip, core = lax.axis_index("z"), lax.axis_index("core")
    q = query.reshape(BLOCK, heads, HEAD_DIM)
    k = k.reshape(-1, HEAD_DIM)
    v = v.reshape(-1, HEAD_DIM)
    scores = jnp.einsum("qhd,kd->hqk", q, k, preferred_element_type=jnp.float32)
    scores = scores / math.sqrt(HEAD_DIM)
    place = jnp.arange(k.shape[0])
    key_core = jnp.where(place < Z * BLOCK, core, 1 - core)
    key_pos = (place // BLOCK % Z * 2 + key_core) * BLOCK + place % BLOCK
    query_pos = (chip * 2 + core) * BLOCK + jnp.arange(BLOCK)
    causal = query_pos[:, None] >= key_pos[None, :]
    scores = jnp.where(causal[None], scores, -1e30)
    top = jnp.max(scores, axis=-1, keepdims=True)
    raised = jnp.exp(scores - top)
    probs = (raised / jnp.sum(raised, axis=-1, keepdims=True)).astype(jnp.bfloat16)
    out = jnp.einsum("hqk,kd->qhd", probs, v, preferred_element_type=jnp.float32)
    return out.reshape(BLOCK, heads * HEAD_DIM)


def ranks_of(ids):
    grid = jnp.arange(EXPERTS, dtype=jnp.int32)
    picked = ids[:, :, None] == grid[None, None, :]
    chosen = jnp.any(picked, axis=1)
    rows = ids.shape[0]
    lower = (jnp.arange(rows)[:, None] > jnp.arange(rows)[None, :]).astype(jnp.bfloat16)
    rank = jnp.dot(lower, chosen.astype(jnp.bfloat16), preferred_element_type=jnp.float32).astype(jnp.int32)
    return jnp.sum(jnp.where(picked, rank[:, None, :], 0), axis=2)


def swap_columns(x):
    return lax.all_to_all(x, E, split_axis=0, concat_axis=0, tiled=True)


def per_device(query, keys, values, resid, route_ids, route_weight, w_in, w_down):
    w_in = lax.all_gather(w_in, "core", axis=0, tiled=True)
    w_down = lax.all_gather(w_down, "core", axis=0, tiled=True)
    k, v = gather_kv(keys, values)
    attended = attend(query, k, v)
    state = (resid.astype(jnp.float32) + attended).astype(jnp.bfloat16)

    ranks = ranks_of(route_ids)
    gates = route_weight / jnp.sum(route_weight, axis=1, keepdims=True)
    sent = jnp.concatenate([state, notes_of(route_ids, ranks, gates)], axis=0)
    plane = lax.all_gather(sent, "z", axis=0)
    plane_slots, plane_gates = read_notes(plane[:, BLOCK:])
    slots_t, gates_t = plane_slots.transpose(0, 2, 1), plane_gates.transpose(0, 2, 1)
    rows = [swap_columns(place_rows(plane_slots, plane, part)) for part in range(PARTS)]
    outs = [experts(part, w_in, w_down) for part in rows]
    outs[0], rows[1] = lax.optimization_barrier((outs[0], rows[1]))
    mixes = [mix_rows(slots_t, gates_t, swap_columns(out), part) for part, out in enumerate(outs)]
    mix = swap_chips(jnp.concatenate(mixes, axis=0))
    mixture = jnp.sum(mix.astype(jnp.float32), axis=0)
    return (state.astype(jnp.float32) + mixture).astype(jnp.bfloat16)


def solution(mesh):
    fine = Mesh(mesh.devices.reshape(4, 4, 16, 2), ("x", "y", "z", "core"))
    placed = (
        P(T, E),
        P(T, None),
        P(T, None),
        P(T, E),
        P(T, None),
        P(T, None),
        P(E, None, T),
        P(E, T, None),
    )
    return jax.shard_map(per_device, mesh=fine, in_specs=placed, out_specs=P(T, E), check_vma=False)
```

```python
import math

import jax
import jax.numpy as jnp
from jax import lax
from jax.experimental import pallas as pl
from jax.experimental.pallas import tpu as pltpu
from jax.sharding import Mesh
from jax.sharding import PartitionSpec as P

HEADS = 32
KV_HEADS = 8
HEAD_DIM = 128
EXPERTS = 16
EXP_CAP = 32
TOPK = 4
BLOCK = 64
WIDTH = 256
Z = 16
PARTS = 2
MIB = 1 << 20

E = ("x", "y")
T = ("z", "core")


def swap_cores(x):
    return lax.ppermute(x, "core", [(0, 1), (1, 0)])


def swap_chips(x):
    return lax.all_to_all(x, "z", split_axis=0, concat_axis=0, tiled=True)


def gather_kv(keys, values):
    first = lax.axis_index(E) // 2 * HEAD_DIM
    k = lax.dynamic_slice_in_dim(keys, first, HEAD_DIM, 1)
    v = lax.dynamic_slice_in_dim(values, first, HEAD_DIM, 1)
    mine = lax.all_gather(jnp.concatenate([k, v], axis=1), "z", axis=0)
    both = jnp.stack([mine, swap_cores(mine)])
    return both[..., :HEAD_DIM], both[..., HEAD_DIM:]


def notes_of(ids, ranks, gates):
    top = lax.reduce_precision(gates, 8, 7)
    rest = gates - top
    middle = lax.reduce_precision(rest, 8, 7)
    low = rest - middle
    parts = [ids.astype(jnp.float32), ranks.astype(jnp.float32), top, middle, low]
    rows = jnp.concatenate([p.T.reshape(1, TOPK * BLOCK) for p in parts], axis=0).astype(jnp.bfloat16)
    return jnp.pad(rows, ((0, 11), (0, 0)))


def read_notes(notes):
    rows = notes[:, :5].astype(jnp.float32).reshape(Z, 5, TOPK, BLOCK)
    return rows[:, 0] * EXP_CAP + rows[:, 1], rows[:, 2] + rows[:, 3] + rows[:, 4]


def in_hbm(x):
    return pltpu.with_memory_space_constraint(x, pltpu.MemorySpace.HBM)


def place_kernel(rows_ref, out_ref):
    for z in range(rows_ref.shape[0]):
        notes = rows_ref[z, BLOCK : BLOCK + 16, :].astype(jnp.float32)
        slots = notes[0:1] * EXP_CAP + notes[1:2]
        grid = lax.broadcasted_iota(jnp.int32, (EXPERTS * EXP_CAP, BLOCK), 0).astype(jnp.float32)
        hit = grid == slots[:, :BLOCK]
        for p in range(1, TOPK):
            hit = jnp.logical_or(hit, grid == slots[:, p * BLOCK : (p + 1) * BLOCK])
        take = jnp.where(hit, 1.0, 0.0).astype(jnp.bfloat16)
        out = jnp.dot(take, rows_ref[z, :BLOCK, :], preferred_element_type=jnp.float32).astype(jnp.bfloat16)
        out_ref[:, z] = out.reshape(EXPERTS, EXP_CAP, WIDTH)


def place_rows(rows, part):
    step = 4
    count = Z // PARTS
    first = part * count // step
    return pl.pallas_call(
        place_kernel,
        grid=(count // step,),
        in_specs=[pl.BlockSpec((step,) + rows.shape[1:], lambda i: (first + i, 0, 0))],
        out_specs=pl.BlockSpec((EXPERTS, step, EXP_CAP, WIDTH), lambda i: (0, i, 0, 0)),
        out_shape=pltpu.MemorySpace.HBM((EXPERTS, count, EXP_CAP, WIDTH), jnp.bfloat16),
        compiler_params=pltpu.CompilerParams(vmem_limit_bytes=(16 if part == 0 else 63) * MIB),
        cost_estimate=pl.CostEstimate(flops=2 * Z * 512 * 64 * 128, bytes_accessed=3 * MIB, transcendentals=0),
    )(rows)


def mix_kernel(slots_ref, gates_ref, rows_ref, out_ref):
    for z in range(slots_ref.shape[0]):
        grid = lax.broadcasted_iota(jnp.int32, (BLOCK, EXPERTS * EXP_CAP), 1).astype(jnp.float32)
        weight = jnp.zeros((BLOCK, EXPERTS * EXP_CAP), jnp.float32)
        for p in range(TOPK):
            weight = jnp.where(grid == slots_ref[z, :, p : p + 1], gates_ref[z, :, p : p + 1], weight)
        high = weight.astype(jnp.bfloat16)
        low = (weight - high.astype(jnp.float32)).astype(jnp.bfloat16)
        rows = rows_ref[:, z].reshape(EXPERTS * EXP_CAP, WIDTH)
        out = jnp.dot(high, rows, preferred_element_type=jnp.float32)
        out += jnp.dot(low, rows, preferred_element_type=jnp.float32)
        out_ref[z] = out.astype(jnp.bfloat16)


def mix_rows(slots, gates, rows, part):
    step = 4
    count = Z // PARTS
    first = part * count // step
    return pl.pallas_call(
        mix_kernel,
        grid=(count // step,),
        in_specs=[
            pl.BlockSpec((step, BLOCK, TOPK), lambda i: (first + i, 0, 0)),
            pl.BlockSpec((step, BLOCK, TOPK), lambda i: (first + i, 0, 0)),
            pl.BlockSpec((EXPERTS, step, EXP_CAP, WIDTH), lambda i: (0, i, 0, 0)),
        ],
        out_specs=pl.BlockSpec((step, BLOCK, WIDTH), lambda i: (i, 0, 0)),
        out_shape=jax.ShapeDtypeStruct((count, BLOCK, WIDTH), jnp.bfloat16),
        compiler_params=pltpu.CompilerParams(vmem_limit_bytes=16 * MIB),
        cost_estimate=pl.CostEstimate(flops=4 * Z * 512 * 64 * 128, bytes_accessed=3 * MIB, transcendentals=0),
    )(slots, gates, rows)


def expert_kernel(rows_ref, in_ref, down_ref, out_ref, raw, normed):
    group = rows_ref.shape[1]
    rows = group * EXP_CAP
    width = EXPERTS * WIDTH
    total = jnp.zeros((rows, WIDTH), jnp.float32)
    for c in range(EXPERTS):
        part = rows_ref[c].reshape(rows, WIDTH).astype(jnp.float32)
        raw[:, c * WIDTH : (c + 1) * WIDTH] = part
        total += part
    center = jnp.sum(total, axis=1, keepdims=True) / width
    spread = jnp.zeros((rows, WIDTH), jnp.float32)
    for c in range(EXPERTS):
        off = raw[:, c * WIDTH : (c + 1) * WIDTH] - center
        spread += off * off
    scale = lax.rsqrt(jnp.sum(spread, axis=1, keepdims=True) / width + 1e-05)
    for c in range(EXPERTS):
        off = raw[:, c * WIDTH : (c + 1) * WIDTH] - center
        normed[:, c * WIDTH : (c + 1) * WIDTH] = (off * scale).astype(jnp.bfloat16)
    hidden = []
    for k in range(2):
        h = jnp.dot(normed[...], in_ref[k], preferred_element_type=jnp.float32)
        hidden.append((h * (1.0 / (1.0 + jnp.exp(-h)))).astype(jnp.bfloat16))
    for c in range(EXPERTS):
        cut = slice(c * WIDTH, (c + 1) * WIDTH)
        out = jnp.dot(hidden[0], down_ref[0, :, cut], preferred_element_type=jnp.float32)
        out += jnp.dot(hidden[1], down_ref[1, :, cut], preferred_element_type=jnp.float32)
        out_ref[c] = out.astype(jnp.bfloat16).reshape(group, EXP_CAP, WIDTH)


def experts(rows, w_in, w_down):
    group = 4
    width = w_down.shape[2]
    count = rows.shape[1]
    spec = pl.BlockSpec((EXPERTS, group, EXP_CAP, WIDTH), lambda i: (0, i, 0, 0))
    return pl.pallas_call(
        expert_kernel,
        grid=(count // group,),
        in_specs=[
            spec,
            pl.BlockSpec(w_in.shape, lambda i: (0, 0, 0), pipeline_mode=pl.Buffered(1)),
            pl.BlockSpec(w_down.shape, lambda i: (0, 0, 0), pipeline_mode=pl.Buffered(1)),
        ],
        out_specs=spec,
        out_shape=pltpu.MemorySpace.HBM(rows.shape, jnp.bfloat16),
        scratch_shapes=[
            pltpu.VMEM((group * EXP_CAP, width), jnp.float32),
            pltpu.VMEM((group * EXP_CAP, width), jnp.bfloat16),
        ],
        compiler_params=pltpu.CompilerParams(vmem_limit_bytes=63 * MIB),
        cost_estimate=pl.CostEstimate(flops=2 * 512 * 512 * width, bytes_accessed=12 * MIB, transcendentals=256 * 512),
    )(in_hbm(rows), in_hbm(w_in), in_hbm(w_down))


def attend(query, k, v):
    heads = query.shape[1] // HEAD_DIM
    chip, core = lax.axis_index("z"), lax.axis_index("core")
    q = query.reshape(BLOCK, heads, HEAD_DIM)
    k = k.reshape(-1, HEAD_DIM)
    v = v.reshape(-1, HEAD_DIM)
    scores = jnp.einsum("qhd,kd->hqk", q, k, preferred_element_type=jnp.float32)
    scores = scores / math.sqrt(HEAD_DIM)
    place = jnp.arange(k.shape[0])
    key_core = jnp.where(place < Z * BLOCK, core, 1 - core)
    key_pos = (place // BLOCK % Z * 2 + key_core) * BLOCK + place % BLOCK
    query_pos = (chip * 2 + core) * BLOCK + jnp.arange(BLOCK)
    causal = query_pos[:, None] >= key_pos[None, :]
    scores = jnp.where(causal[None], scores, -1e30)
    top = jnp.max(scores, axis=-1, keepdims=True)
    raised = jnp.exp(scores - top)
    probs = (raised / jnp.sum(raised, axis=-1, keepdims=True)).astype(jnp.bfloat16)
    out = jnp.einsum("hqk,kd->qhd", probs, v, preferred_element_type=jnp.float32)
    return out.reshape(BLOCK, heads * HEAD_DIM)


def ranks_of(ids):
    grid = jnp.arange(EXPERTS, dtype=jnp.int32)
    picked = ids[:, :, None] == grid[None, None, :]
    chosen = jnp.any(picked, axis=1)
    rows = ids.shape[0]
    lower = (jnp.arange(rows)[:, None] > jnp.arange(rows)[None, :]).astype(jnp.bfloat16)
    rank = jnp.dot(lower, chosen.astype(jnp.bfloat16), preferred_element_type=jnp.float32).astype(jnp.int32)
    return jnp.sum(jnp.where(picked, rank[:, None, :], 0), axis=2)


def swap_columns(x):
    return lax.all_to_all(x, E, split_axis=0, concat_axis=0, tiled=True)


def per_device(query, keys, values, resid, route_ids, route_weight, w_in, w_down):
    w_in = lax.all_gather(w_in, "core", axis=0, tiled=True)
    w_down = lax.all_gather(w_down, "core", axis=0, tiled=True)
    k, v = gather_kv(keys, values)
    attended = attend(query, k, v)
    state = (resid.astype(jnp.float32) + attended).astype(jnp.bfloat16)

    ranks = ranks_of(route_ids)
    gates = route_weight / jnp.sum(route_weight, axis=1, keepdims=True)
    sent = jnp.concatenate([state, notes_of(route_ids, ranks, gates)], axis=0)
    plane = lax.all_gather(sent, "z", axis=0)
    plane_slots, plane_gates = read_notes(plane[:, BLOCK:])
    slots_t, gates_t = plane_slots.transpose(0, 2, 1), plane_gates.transpose(0, 2, 1)
    rows = [swap_columns(place_rows(plane, part)) for part in range(PARTS)]
    outs = [experts(part, w_in, w_down) for part in rows]
    outs[0], rows[1] = lax.optimization_barrier((outs[0], rows[1]))
    mixes = [mix_rows(slots_t, gates_t, swap_columns(out), part) for part, out in enumerate(outs)]
    mix = swap_chips(jnp.concatenate(mixes, axis=0))
    mixture = jnp.sum(mix.astype(jnp.float32), axis=0)
    return (state.astype(jnp.float32) + mixture).astype(jnp.bfloat16)


def solution(mesh):
    fine = Mesh(mesh.devices.reshape(4, 4, 16, 2), ("x", "y", "z", "core"))
    placed = (
        P(T, E),
        P(T, None),
        P(T, None),
        P(T, E),
        P(T, None),
        P(T, None),
        P(E, None, T),
        P(E, T, None),
    )
    return jax.shard_map(per_device, mesh=fine, in_specs=placed, out_specs=P(T, E), check_vma=False)
```

```python
import math

import jax
import jax.numpy as jnp
from jax import lax
from jax.experimental import pallas as pl
from jax.experimental.pallas import tpu as pltpu
from jax.sharding import Mesh
from jax.sharding import PartitionSpec as P

HEADS = 32
KV_HEADS = 8
HEAD_DIM = 128
EXPERTS = 16
EXP_CAP = 32
TOPK = 4
BLOCK = 64
WIDTH = 256
Z = 16
PARTS = 2
MIB = 1 << 20

E = ("x", "y")
T = ("z", "core")


def swap_cores(x):
    return lax.ppermute(x, "core", [(0, 1), (1, 0)])


def fold(x, bit):
    mine = (lax.axis_index("z") >> bit) & 1
    pairs = x.reshape((x.shape[0] // 2, 2) + x.shape[1:])
    kept = lax.dynamic_index_in_dim(pairs, mine, 1, keepdims=False)
    sent = lax.dynamic_index_in_dim(pairs, 1 - mine, 1, keepdims=False)
    came = lax.ppermute(sent, "z", [(i, i ^ (1 << bit)) for i in range(Z)])
    return (kept.astype(jnp.float32) + came.astype(jnp.float32)).astype(x.dtype)


def join(lower, upper):
    high = lax.axis_index("z") >= Z // 2
    kept, sent = jnp.where(high, upper, lower), jnp.where(high, lower, upper)
    came = lax.ppermute(sent, "z", [(i, i ^ 8) for i in range(Z)])
    return kept[0].astype(jnp.float32) + came[0].astype(jnp.float32)


def gather_kv(keys, values):
    first = lax.axis_index(E) // 2 * HEAD_DIM
    k = lax.dynamic_slice_in_dim(keys, first, HEAD_DIM, 1)
    v = lax.dynamic_slice_in_dim(values, first, HEAD_DIM, 1)
    mine = lax.all_gather(jnp.concatenate([k, v], axis=1), "z", axis=0)
    both = jnp.stack([mine, swap_cores(mine)])
    return both[..., :HEAD_DIM], both[..., HEAD_DIM:]


def notes_of(ids, ranks, gates):
    top = lax.reduce_precision(gates, 8, 7)
    rest = gates - top
    middle = lax.reduce_precision(rest, 8, 7)
    low = rest - middle
    parts = [ids.astype(jnp.float32), ranks.astype(jnp.float32), top, middle, low]
    rows = jnp.concatenate([p.T.reshape(1, TOPK * BLOCK) for p in parts], axis=0).astype(jnp.bfloat16)
    return jnp.pad(rows, ((0, 11), (0, 0)))


def read_notes(notes):
    rows = notes[:, :5].astype(jnp.float32).reshape(Z, 5, TOPK, BLOCK)
    return rows[:, 0] * EXP_CAP + rows[:, 1], rows[:, 2] + rows[:, 3] + rows[:, 4]


def in_hbm(x):
    return pltpu.with_memory_space_constraint(x, pltpu.MemorySpace.HBM)


def place_kernel(rows_ref, out_ref):
    for z in range(rows_ref.shape[0]):
        notes = rows_ref[z, BLOCK : BLOCK + 16, :].astype(jnp.float32)
        slots = notes[0:1] * EXP_CAP + notes[1:2]
        grid = lax.broadcasted_iota(jnp.int32, (EXPERTS * EXP_CAP, BLOCK), 0).astype(jnp.float32)
        hit = grid == slots[:, :BLOCK]
        for p in range(1, TOPK):
            hit = jnp.logical_or(hit, grid == slots[:, p * BLOCK : (p + 1) * BLOCK])
        take = jnp.where(hit, 1.0, 0.0).astype(jnp.bfloat16)
        out = jnp.dot(take, rows_ref[z, :BLOCK, :], preferred_element_type=jnp.float32).astype(jnp.bfloat16)
        out_ref[:, z] = out.reshape(EXPERTS, EXP_CAP, WIDTH)


def place_rows(rows, part):
    step = 4
    count = Z // PARTS
    first = part * count // step
    return pl.pallas_call(
        place_kernel,
        grid=(count // step,),
        in_specs=[pl.BlockSpec((step,) + rows.shape[1:], lambda i: (first + i, 0, 0))],
        out_specs=pl.BlockSpec((EXPERTS, step, EXP_CAP, WIDTH), lambda i: (0, i, 0, 0)),
        out_shape=pltpu.MemorySpace.HBM((EXPERTS, count, EXP_CAP, WIDTH), jnp.bfloat16),
        compiler_params=pltpu.CompilerParams(vmem_limit_bytes=(16 if part == 0 else 63) * MIB),
        cost_estimate=pl.CostEstimate(flops=2 * Z * 512 * 64 * 128, bytes_accessed=3 * MIB, transcendentals=0),
    )(rows)


def mix_kernel(slots_ref, gates_ref, rows_ref, out_ref):
    for z in range(slots_ref.shape[0]):
        grid = lax.broadcasted_iota(jnp.int32, (BLOCK, EXPERTS * EXP_CAP), 1).astype(jnp.float32)
        weight = jnp.zeros((BLOCK, EXPERTS * EXP_CAP), jnp.float32)
        for p in range(TOPK):
            weight = jnp.where(grid == slots_ref[z, :, p : p + 1], gates_ref[z, :, p : p + 1], weight)
        high = weight.astype(jnp.bfloat16)
        low = (weight - high.astype(jnp.float32)).astype(jnp.bfloat16)
        rows = rows_ref[:, z].reshape(EXPERTS * EXP_CAP, WIDTH)
        out = jnp.dot(high, rows, preferred_element_type=jnp.float32)
        out += jnp.dot(low, rows, preferred_element_type=jnp.float32)
        out_ref[z] = out.astype(jnp.bfloat16)


def mix_rows(slots, gates, rows, part):
    step = 4
    count = Z // PARTS
    first = part * count // step
    return pl.pallas_call(
        mix_kernel,
        grid=(count // step,),
        in_specs=[
            pl.BlockSpec((step, BLOCK, TOPK), lambda i: (first + i, 0, 0)),
            pl.BlockSpec((step, BLOCK, TOPK), lambda i: (first + i, 0, 0)),
            pl.BlockSpec((EXPERTS, step, EXP_CAP, WIDTH), lambda i: (0, i, 0, 0)),
        ],
        out_specs=pl.BlockSpec((step, BLOCK, WIDTH), lambda i: (i, 0, 0)),
        out_shape=jax.ShapeDtypeStruct((count, BLOCK, WIDTH), jnp.bfloat16),
        compiler_params=pltpu.CompilerParams(vmem_limit_bytes=16 * MIB),
        cost_estimate=pl.CostEstimate(flops=4 * Z * 512 * 64 * 128, bytes_accessed=3 * MIB, transcendentals=0),
    )(slots, gates, rows)


def expert_kernel(rows_ref, in_ref, down_ref, out_ref, raw, normed):
    group = rows_ref.shape[1]
    rows = group * EXP_CAP
    width = EXPERTS * WIDTH
    total = jnp.zeros((rows, WIDTH), jnp.float32)
    for c in range(EXPERTS):
        part = rows_ref[c].reshape(rows, WIDTH).astype(jnp.float32)
        raw[:, c * WIDTH : (c + 1) * WIDTH] = part
        total += part
    center = jnp.sum(total, axis=1, keepdims=True) / width
    spread = jnp.zeros((rows, WIDTH), jnp.float32)
    for c in range(EXPERTS):
        off = raw[:, c * WIDTH : (c + 1) * WIDTH] - center
        spread += off * off
    scale = lax.rsqrt(jnp.sum(spread, axis=1, keepdims=True) / width + 1e-05)
    for c in range(EXPERTS):
        off = raw[:, c * WIDTH : (c + 1) * WIDTH] - center
        normed[:, c * WIDTH : (c + 1) * WIDTH] = (off * scale).astype(jnp.bfloat16)
    hidden = []
    for k in range(2):
        h = jnp.dot(normed[...], in_ref[k], preferred_element_type=jnp.float32)
        hidden.append((h * (1.0 / (1.0 + jnp.exp(-h)))).astype(jnp.bfloat16))
    for c in range(EXPERTS):
        cut = slice(c * WIDTH, (c + 1) * WIDTH)
        out = jnp.dot(hidden[0], down_ref[0, :, cut], preferred_element_type=jnp.float32)
        out += jnp.dot(hidden[1], down_ref[1, :, cut], preferred_element_type=jnp.float32)
        out_ref[c] = out.astype(jnp.bfloat16).reshape(group, EXP_CAP, WIDTH)


def experts(rows, w_in, w_down):
    group = 4
    width = w_down.shape[2]
    count = rows.shape[1]
    spec = pl.BlockSpec((EXPERTS, group, EXP_CAP, WIDTH), lambda i: (0, i, 0, 0))
    return pl.pallas_call(
        expert_kernel,
        grid=(count // group,),
        in_specs=[
            spec,
            pl.BlockSpec(w_in.shape, lambda i: (0, 0, 0), pipeline_mode=pl.Buffered(1)),
            pl.BlockSpec(w_down.shape, lambda i: (0, 0, 0), pipeline_mode=pl.Buffered(1)),
        ],
        out_specs=spec,
        out_shape=pltpu.MemorySpace.HBM(rows.shape, jnp.bfloat16),
        scratch_shapes=[
            pltpu.VMEM((group * EXP_CAP, width), jnp.float32),
            pltpu.VMEM((group * EXP_CAP, width), jnp.bfloat16),
        ],
        compiler_params=pltpu.CompilerParams(vmem_limit_bytes=63 * MIB),
        cost_estimate=pl.CostEstimate(flops=2 * 512 * 512 * width, bytes_accessed=12 * MIB, transcendentals=256 * 512),
    )(in_hbm(rows), in_hbm(w_in), in_hbm(w_down))


def attend(query, k, v):
    heads = query.shape[1] // HEAD_DIM
    chip, core = lax.axis_index("z"), lax.axis_index("core")
    q = query.reshape(BLOCK, heads, HEAD_DIM)
    k = k.reshape(-1, HEAD_DIM)
    v = v.reshape(-1, HEAD_DIM)
    scores = jnp.einsum("qhd,kd->hqk", q, k, preferred_element_type=jnp.float32)
    scores = scores / math.sqrt(HEAD_DIM)
    place = jnp.arange(k.shape[0])
    key_core = jnp.where(place < Z * BLOCK, core, 1 - core)
    key_pos = (place // BLOCK % Z * 2 + key_core) * BLOCK + place % BLOCK
    query_pos = (chip * 2 + core) * BLOCK + jnp.arange(BLOCK)
    causal = query_pos[:, None] >= key_pos[None, :]
    scores = jnp.where(causal[None], scores, -1e30)
    top = jnp.max(scores, axis=-1, keepdims=True)
    raised = jnp.exp(scores - top)
    probs = (raised / jnp.sum(raised, axis=-1, keepdims=True)).astype(jnp.bfloat16)
    out = jnp.einsum("hqk,kd->qhd", probs, v, preferred_element_type=jnp.float32)
    return out.reshape(BLOCK, heads * HEAD_DIM)


def ranks_of(ids):
    grid = jnp.arange(EXPERTS, dtype=jnp.int32)
    picked = ids[:, :, None] == grid[None, None, :]
    chosen = jnp.any(picked, axis=1)
    rows = ids.shape[0]
    lower = (jnp.arange(rows)[:, None] > jnp.arange(rows)[None, :]).astype(jnp.bfloat16)
    rank = jnp.dot(lower, chosen.astype(jnp.bfloat16), preferred_element_type=jnp.float32).astype(jnp.int32)
    return jnp.sum(jnp.where(picked, rank[:, None, :], 0), axis=2)


def swap_columns(x):
    return lax.all_to_all(x, E, split_axis=0, concat_axis=0, tiled=True)


def per_device(query, keys, values, resid, route_ids, route_weight, w_in, w_down):
    w_in = lax.all_gather(w_in, "core", axis=0, tiled=True)
    w_down = lax.all_gather(w_down, "core", axis=0, tiled=True)
    k, v = gather_kv(keys, values)
    attended = attend(query, k, v)
    state = (resid.astype(jnp.float32) + attended).astype(jnp.bfloat16)

    ranks = ranks_of(route_ids)
    gates = route_weight / jnp.sum(route_weight, axis=1, keepdims=True)
    sent = jnp.concatenate([state, notes_of(route_ids, ranks, gates)], axis=0)
    plane = lax.all_gather(sent, "z", axis=0)
    plane_slots, plane_gates = read_notes(plane[:, BLOCK:])
    slots_t, gates_t = plane_slots.transpose(0, 2, 1), plane_gates.transpose(0, 2, 1)
    first = swap_columns(place_rows(plane, 0))
    second, first = lax.optimization_barrier((place_rows(plane, 1), first))
    second = swap_columns(second)
    out = experts(first, w_in, w_down)
    out, second, slots_t, gates_t = lax.optimization_barrier((out, second, slots_t, gates_t))
    first = swap_columns(out)
    out, first = lax.optimization_barrier((experts(second, w_in, w_down), first))
    second = swap_columns(out)
    lower = fold(fold(mix_rows(slots_t, gates_t, first, 0), 0), 1)
    lower, second = lax.optimization_barrier((lower, second))
    upper = fold(fold(mix_rows(slots_t, gates_t, second, 1), 0), 1)
    mixture = join(fold(lower, 2), fold(upper, 2))
    return (state.astype(jnp.float32) + mixture).astype(jnp.bfloat16)


def solution(mesh):
    fine = Mesh(mesh.devices.reshape(4, 4, 16, 2), ("x", "y", "z", "core"))
    placed = (
        P(T, E),
        P(T, None),
        P(T, None),
        P(T, E),
        P(T, None),
        P(T, None),
        P(E, None, T),
        P(E, T, None),
    )
    return jax.shard_map(per_device, mesh=fine, in_specs=placed, out_specs=P(T, E), check_vma=False)
```

```python
import math

import jax
import jax.numpy as jnp
from jax import lax
from jax.experimental import pallas as pl
from jax.experimental.pallas import tpu as pltpu
from jax.sharding import Mesh
from jax.sharding import PartitionSpec as P

HEADS = 32
KV_HEADS = 8
HEAD_DIM = 128
EXPERTS = 16
EXP_CAP = 32
TOPK = 4
BLOCK = 64
WIDTH = 256
Z = 16
PARTS = 2
MIB = 1 << 20

E = ("x", "y")
T = ("z", "core")


def swap_cores(x):
    return lax.ppermute(x, "core", [(0, 1), (1, 0)])


def sum_chips(x):
    up = [2 * z for z in range(Z)]
    down = [2 * z + 1 for z in reversed(range(Z))]
    x = jnp.where(lax.axis_index("core") == 0, x, x[::-1])
    came = lax.all_to_all(x, T, split_axis=0, concat_axis=0, axis_index_groups=[up, down], tiled=True)
    return jnp.sum(came.astype(jnp.float32), axis=0)


def gather_kv(keys, values):
    first = lax.axis_index(E) // 2 * HEAD_DIM
    k = lax.dynamic_slice_in_dim(keys, first, HEAD_DIM, 1)
    v = lax.dynamic_slice_in_dim(values, first, HEAD_DIM, 1)
    mine = lax.all_gather(jnp.concatenate([k, v], axis=1), "z", axis=0)
    both = jnp.stack([mine, swap_cores(mine)])
    return both[..., :HEAD_DIM], both[..., HEAD_DIM:]


def notes_of(ids, ranks, gates):
    top = lax.reduce_precision(gates, 8, 7)
    rest = gates - top
    middle = lax.reduce_precision(rest, 8, 7)
    low = rest - middle
    parts = [ids.astype(jnp.float32), ranks.astype(jnp.float32), top, middle, low]
    rows = jnp.concatenate([p.T.reshape(1, TOPK * BLOCK) for p in parts], axis=0).astype(jnp.bfloat16)
    return jnp.pad(rows, ((0, 11), (0, 0)))


def read_notes(notes):
    rows = notes[:, :5].astype(jnp.float32).reshape(Z, 5, TOPK, BLOCK)
    return rows[:, 0] * EXP_CAP + rows[:, 1], rows[:, 2] + rows[:, 3] + rows[:, 4]


def in_hbm(x):
    return pltpu.with_memory_space_constraint(x, pltpu.MemorySpace.HBM)


def place_kernel(rows_ref, out_ref):
    for z in range(rows_ref.shape[0]):
        notes = rows_ref[z, BLOCK : BLOCK + 16, :].astype(jnp.float32)
        slots = notes[0:1] * EXP_CAP + notes[1:2]
        grid = lax.broadcasted_iota(jnp.int32, (EXPERTS * EXP_CAP, BLOCK), 0).astype(jnp.float32)
        hit = grid == slots[:, :BLOCK]
        for p in range(1, TOPK):
            hit = jnp.logical_or(hit, grid == slots[:, p * BLOCK : (p + 1) * BLOCK])
        take = jnp.where(hit, 1.0, 0.0).astype(jnp.bfloat16)
        out = jnp.dot(take, rows_ref[z, :BLOCK, :], preferred_element_type=jnp.float32).astype(jnp.bfloat16)
        out_ref[:, z] = out.reshape(EXPERTS, EXP_CAP, WIDTH)


def place_rows(rows, part):
    step = 4
    count = Z // PARTS
    first = part * count // step
    return pl.pallas_call(
        place_kernel,
        grid=(count // step,),
        in_specs=[pl.BlockSpec((step,) + rows.shape[1:], lambda i: (first + i, 0, 0))],
        out_specs=pl.BlockSpec((EXPERTS, step, EXP_CAP, WIDTH), lambda i: (0, i, 0, 0)),
        out_shape=pltpu.MemorySpace.HBM((EXPERTS, count, EXP_CAP, WIDTH), jnp.bfloat16),
        compiler_params=pltpu.CompilerParams(vmem_limit_bytes=(16 if part == 0 else 63) * MIB),
        cost_estimate=pl.CostEstimate(flops=2 * Z * 512 * 64 * 128, bytes_accessed=3 * MIB, transcendentals=0),
    )(rows)


def mix_kernel(slots_ref, gates_ref, rows_ref, out_ref):
    for z in range(slots_ref.shape[0]):
        grid = lax.broadcasted_iota(jnp.int32, (BLOCK, EXPERTS * EXP_CAP), 1).astype(jnp.float32)
        weight = jnp.zeros((BLOCK, EXPERTS * EXP_CAP), jnp.float32)
        for p in range(TOPK):
            weight = jnp.where(grid == slots_ref[z, :, p : p + 1], gates_ref[z, :, p : p + 1], weight)
        high = weight.astype(jnp.bfloat16)
        low = (weight - high.astype(jnp.float32)).astype(jnp.bfloat16)
        rows = rows_ref[:, z].reshape(EXPERTS * EXP_CAP, WIDTH)
        out = jnp.dot(high, rows, preferred_element_type=jnp.float32)
        out += jnp.dot(low, rows, preferred_element_type=jnp.float32)
        out_ref[z] = out.astype(jnp.bfloat16)


def mix_rows(slots, gates, rows, part):
    step = 4
    count = Z // PARTS
    first = part * count // step
    return pl.pallas_call(
        mix_kernel,
        grid=(count // step,),
        in_specs=[
            pl.BlockSpec((step, BLOCK, TOPK), lambda i: (first + i, 0, 0)),
            pl.BlockSpec((step, BLOCK, TOPK), lambda i: (first + i, 0, 0)),
            pl.BlockSpec((EXPERTS, step, EXP_CAP, WIDTH), lambda i: (0, i, 0, 0)),
        ],
        out_specs=pl.BlockSpec((step, BLOCK, WIDTH), lambda i: (i, 0, 0)),
        out_shape=jax.ShapeDtypeStruct((count, BLOCK, WIDTH), jnp.bfloat16),
        compiler_params=pltpu.CompilerParams(vmem_limit_bytes=16 * MIB),
        cost_estimate=pl.CostEstimate(flops=4 * Z * 512 * 64 * 128, bytes_accessed=3 * MIB, transcendentals=0),
    )(slots, gates, rows)


def expert_kernel(rows_ref, in_ref, down_ref, out_ref, raw, normed):
    group = rows_ref.shape[1]
    rows = group * EXP_CAP
    width = EXPERTS * WIDTH
    total = jnp.zeros((rows, WIDTH), jnp.float32)
    for c in range(EXPERTS):
        part = rows_ref[c].reshape(rows, WIDTH).astype(jnp.float32)
        raw[:, c * WIDTH : (c + 1) * WIDTH] = part
        total += part
    center = jnp.sum(total, axis=1, keepdims=True) / width
    spread = jnp.zeros((rows, WIDTH), jnp.float32)
    for c in range(EXPERTS):
        off = raw[:, c * WIDTH : (c + 1) * WIDTH] - center
        spread += off * off
    scale = lax.rsqrt(jnp.sum(spread, axis=1, keepdims=True) / width + 1e-05)
    for c in range(EXPERTS):
        off = raw[:, c * WIDTH : (c + 1) * WIDTH] - center
        normed[:, c * WIDTH : (c + 1) * WIDTH] = (off * scale).astype(jnp.bfloat16)
    hidden = []
    for k in range(2):
        h = jnp.dot(normed[...], in_ref[k], preferred_element_type=jnp.float32)
        hidden.append((h * (1.0 / (1.0 + jnp.exp(-h)))).astype(jnp.bfloat16))
    for c in range(EXPERTS):
        cut = slice(c * WIDTH, (c + 1) * WIDTH)
        out = jnp.dot(hidden[0], down_ref[0, :, cut], preferred_element_type=jnp.float32)
        out += jnp.dot(hidden[1], down_ref[1, :, cut], preferred_element_type=jnp.float32)
        out_ref[c] = out.astype(jnp.bfloat16).reshape(group, EXP_CAP, WIDTH)


def experts(rows, w_in, w_down):
    group = 4
    width = w_down.shape[2]
    count = rows.shape[1]
    spec = pl.BlockSpec((EXPERTS, group, EXP_CAP, WIDTH), lambda i: (0, i, 0, 0))
    return pl.pallas_call(
        expert_kernel,
        grid=(count // group,),
        in_specs=[
            spec,
            pl.BlockSpec(w_in.shape, lambda i: (0, 0, 0), pipeline_mode=pl.Buffered(1)),
            pl.BlockSpec(w_down.shape, lambda i: (0, 0, 0), pipeline_mode=pl.Buffered(1)),
        ],
        out_specs=spec,
        out_shape=pltpu.MemorySpace.HBM(rows.shape, jnp.bfloat16),
        scratch_shapes=[
            pltpu.VMEM((group * EXP_CAP, width), jnp.float32),
            pltpu.VMEM((group * EXP_CAP, width), jnp.bfloat16),
        ],
        compiler_params=pltpu.CompilerParams(vmem_limit_bytes=63 * MIB),
        cost_estimate=pl.CostEstimate(flops=2 * 512 * 512 * width, bytes_accessed=12 * MIB, transcendentals=256 * 512),
    )(in_hbm(rows), in_hbm(w_in), in_hbm(w_down))


def attend(query, k, v):
    heads = query.shape[1] // HEAD_DIM
    chip, core = lax.axis_index("z"), lax.axis_index("core")
    q = query.reshape(BLOCK, heads, HEAD_DIM)
    k = k.reshape(-1, HEAD_DIM)
    v = v.reshape(-1, HEAD_DIM)
    scores = jnp.einsum("qhd,kd->hqk", q, k, preferred_element_type=jnp.float32)
    scores = scores / math.sqrt(HEAD_DIM)
    place = jnp.arange(k.shape[0])
    key_core = jnp.where(place < Z * BLOCK, core, 1 - core)
    key_pos = (place // BLOCK % Z * 2 + key_core) * BLOCK + place % BLOCK
    query_pos = (chip * 2 + core) * BLOCK + jnp.arange(BLOCK)
    causal = query_pos[:, None] >= key_pos[None, :]
    scores = jnp.where(causal[None], scores, -1e30)
    top = jnp.max(scores, axis=-1, keepdims=True)
    raised = jnp.exp(scores - top)
    probs = (raised / jnp.sum(raised, axis=-1, keepdims=True)).astype(jnp.bfloat16)
    out = jnp.einsum("hqk,kd->qhd", probs, v, preferred_element_type=jnp.float32)
    return out.reshape(BLOCK, heads * HEAD_DIM)


def ranks_of(ids):
    grid = jnp.arange(EXPERTS, dtype=jnp.int32)
    picked = ids[:, :, None] == grid[None, None, :]
    chosen = jnp.any(picked, axis=1)
    rows = ids.shape[0]
    lower = (jnp.arange(rows)[:, None] > jnp.arange(rows)[None, :]).astype(jnp.bfloat16)
    rank = jnp.dot(lower, chosen.astype(jnp.bfloat16), preferred_element_type=jnp.float32).astype(jnp.int32)
    return jnp.sum(jnp.where(picked, rank[:, None, :], 0), axis=2)


def swap_columns(x):
    return lax.all_to_all(x, E, split_axis=0, concat_axis=0, tiled=True)


def per_device(query, keys, values, resid, route_ids, route_weight, w_in, w_down):
    w_in = lax.all_gather(w_in, "core", axis=0, tiled=True)
    w_down = lax.all_gather(w_down, "core", axis=0, tiled=True)
    k, v = gather_kv(keys, values)
    attended = attend(query, k, v)
    state = (resid.astype(jnp.float32) + attended).astype(jnp.bfloat16)

    ranks = ranks_of(route_ids)
    gates = route_weight / jnp.sum(route_weight, axis=1, keepdims=True)
    sent = jnp.concatenate([state, notes_of(route_ids, ranks, gates)], axis=0)
    plane = lax.all_gather(sent, "z", axis=0)
    plane_slots, plane_gates = read_notes(plane[:, BLOCK:])
    slots_t, gates_t = plane_slots.transpose(0, 2, 1), plane_gates.transpose(0, 2, 1)
    rows = [swap_columns(place_rows(plane, part)) for part in range(PARTS)]
    outs = [experts(part, w_in, w_down) for part in rows]
    outs[0], rows[1] = lax.optimization_barrier((outs[0], rows[1]))
    mixes = [mix_rows(slots_t, gates_t, swap_columns(out), part) for part, out in enumerate(outs)]
    mixture = sum_chips(jnp.concatenate(mixes, axis=0))
    return (state.astype(jnp.float32) + mixture).astype(jnp.bfloat16)


def solution(mesh):
    fine = Mesh(mesh.devices.reshape(4, 4, 16, 2), ("x", "y", "z", "core"))
    placed = (
        P(T, E),
        P(T, None),
        P(T, None),
        P(T, E),
        P(T, None),
        P(T, None),
        P(E, None, T),
        P(E, T, None),
    )
    return jax.shard_map(per_device, mesh=fine, in_specs=placed, out_specs=P(T, E), check_vma=False)
```

```python
import math

import jax
import jax.numpy as jnp
from jax import lax
from jax.experimental import pallas as pl
from jax.experimental.pallas import tpu as pltpu
from jax.sharding import Mesh
from jax.sharding import PartitionSpec as P

HEADS = 32
KV_HEADS = 8
HEAD_DIM = 128
EXPERTS = 16
EXP_CAP = 32
TOPK = 4
BLOCK = 64
WIDTH = 256
Z = 16
PARTS = 2
MIB = 1 << 20

E = ("x", "y")
T = ("z", "core")


def swap_cores(x):
    return lax.ppermute(x, "core", [(0, 1), (1, 0)])


def swap_chips(x):
    return lax.all_to_all(x, "z", split_axis=0, concat_axis=0, tiled=True)


def gather_kv(keys, values):
    first = lax.axis_index(E) // 2 * HEAD_DIM
    k = lax.dynamic_slice_in_dim(keys, first, HEAD_DIM, 1)
    v = lax.dynamic_slice_in_dim(values, first, HEAD_DIM, 1)
    mine = lax.all_gather(jnp.concatenate([k, v], axis=1), "z", axis=0)
    both = jnp.stack([mine, swap_cores(mine)])
    return both[..., :HEAD_DIM], both[..., HEAD_DIM:]


def notes_of(ids, ranks, gates):
    top = lax.reduce_precision(gates, 8, 7)
    rest = gates - top
    middle = lax.reduce_precision(rest, 8, 7)
    low = rest - middle
    parts = [ids.astype(jnp.float32), ranks.astype(jnp.float32), top, middle, low]
    rows = jnp.concatenate([p.T.reshape(1, TOPK * BLOCK) for p in parts], axis=0).astype(jnp.bfloat16)
    return jnp.pad(rows, ((0, 11), (0, 0)))


def read_notes(notes):
    rows = notes[:, :5].astype(jnp.float32).reshape(Z, 5, TOPK, BLOCK)
    return rows[:, 0] * EXP_CAP + rows[:, 1], rows[:, 2] + rows[:, 3] + rows[:, 4]


def in_hbm(x):
    return pltpu.with_memory_space_constraint(x, pltpu.MemorySpace.HBM)


def place_kernel(rows_ref, out_ref):
    for z in range(rows_ref.shape[0]):
        notes = rows_ref[z, BLOCK : BLOCK + 16, :].astype(jnp.float32)
        slots = notes[0:1] * EXP_CAP + notes[1:2]
        grid = lax.broadcasted_iota(jnp.int32, (EXPERTS * EXP_CAP, BLOCK), 0).astype(jnp.float32)
        hit = grid == slots[:, :BLOCK]
        for p in range(1, TOPK):
            hit = jnp.logical_or(hit, grid == slots[:, p * BLOCK : (p + 1) * BLOCK])
        take = jnp.where(hit, 1.0, 0.0).astype(jnp.bfloat16)
        out = jnp.dot(take, rows_ref[z, :BLOCK, :], preferred_element_type=jnp.float32).astype(jnp.bfloat16)
        out_ref[:, z] = out.reshape(EXPERTS, EXP_CAP, WIDTH)


def place_rows(rows, part):
    step = 4
    count = Z // PARTS
    first = part * count // step
    return pl.pallas_call(
        place_kernel,
        grid=(count // step,),
        in_specs=[pl.BlockSpec((step,) + rows.shape[1:], lambda i: (first + i, 0, 0))],
        out_specs=pl.BlockSpec((EXPERTS, step, EXP_CAP, WIDTH), lambda i: (0, i, 0, 0)),
        out_shape=pltpu.MemorySpace.HBM((EXPERTS, count, EXP_CAP, WIDTH), jnp.bfloat16),
        compiler_params=pltpu.CompilerParams(vmem_limit_bytes=(16 if part == 0 else 63) * MIB),
        cost_estimate=pl.CostEstimate(flops=2 * Z * 512 * 64 * 128, bytes_accessed=3 * MIB, transcendentals=0),
    )(rows)


def mix_kernel(slots_ref, gates_ref, rows_ref, out_ref):
    for z in range(slots_ref.shape[0]):
        grid = lax.broadcasted_iota(jnp.int32, (BLOCK, EXPERTS * EXP_CAP), 1).astype(jnp.float32)
        weight = jnp.zeros((BLOCK, EXPERTS * EXP_CAP), jnp.float32)
        for p in range(TOPK):
            weight = jnp.where(grid == slots_ref[z, :, p : p + 1], gates_ref[z, :, p : p + 1], weight)
        high = weight.astype(jnp.bfloat16)
        low = (weight - high.astype(jnp.float32)).astype(jnp.bfloat16)
        rows = rows_ref[:, z].reshape(EXPERTS * EXP_CAP, WIDTH)
        out = jnp.dot(high, rows, preferred_element_type=jnp.float32)
        out += jnp.dot(low, rows, preferred_element_type=jnp.float32)
        out_ref[z] = out.astype(jnp.bfloat16)


def mix_rows(slots, gates, rows, part):
    step = 4
    count = Z // PARTS
    first = part * count // step
    return pl.pallas_call(
        mix_kernel,
        grid=(count // step,),
        in_specs=[
            pl.BlockSpec((step, BLOCK, TOPK), lambda i: (first + i, 0, 0)),
            pl.BlockSpec((step, BLOCK, TOPK), lambda i: (first + i, 0, 0)),
            pl.BlockSpec((EXPERTS, step, EXP_CAP, WIDTH), lambda i: (0, i, 0, 0)),
        ],
        out_specs=pl.BlockSpec((step, BLOCK, WIDTH), lambda i: (i, 0, 0)),
        out_shape=jax.ShapeDtypeStruct((count, BLOCK, WIDTH), jnp.bfloat16),
        compiler_params=pltpu.CompilerParams(vmem_limit_bytes=32 * MIB),
        cost_estimate=pl.CostEstimate(flops=4 * Z * 512 * 64 * 128, bytes_accessed=3 * MIB, transcendentals=0),
    )(slots, gates, in_hbm(rows))


def expert_kernel(rows_ref, in_ref, down_ref, out_ref, raw, normed):
    group = rows_ref.shape[1]
    rows = group * EXP_CAP
    width = EXPERTS * WIDTH
    total = jnp.zeros((rows, WIDTH), jnp.float32)
    for c in range(EXPERTS):
        part = rows_ref[c].reshape(rows, WIDTH).astype(jnp.float32)
        raw[:, c * WIDTH : (c + 1) * WIDTH] = part
        total += part
    center = jnp.sum(total, axis=1, keepdims=True) / width
    spread = jnp.zeros((rows, WIDTH), jnp.float32)
    for c in range(EXPERTS):
        off = raw[:, c * WIDTH : (c + 1) * WIDTH] - center
        spread += off * off
    scale = lax.rsqrt(jnp.sum(spread, axis=1, keepdims=True) / width + 1e-05)
    for c in range(EXPERTS):
        off = raw[:, c * WIDTH : (c + 1) * WIDTH] - center
        normed[:, c * WIDTH : (c + 1) * WIDTH] = (off * scale).astype(jnp.bfloat16)
    hidden = []
    for k in range(2):
        h = jnp.dot(normed[...], in_ref[k], preferred_element_type=jnp.float32)
        hidden.append((h * (1.0 / (1.0 + jnp.exp(-h)))).astype(jnp.bfloat16))
    for c in range(EXPERTS):
        cut = slice(c * WIDTH, (c + 1) * WIDTH)
        out = jnp.dot(hidden[0], down_ref[0, :, cut], preferred_element_type=jnp.float32)
        out += jnp.dot(hidden[1], down_ref[1, :, cut], preferred_element_type=jnp.float32)
        out_ref[c] = out.astype(jnp.bfloat16).reshape(group, EXP_CAP, WIDTH)


def experts(rows, w_in, w_down):
    group = 4
    width = w_down.shape[2]
    count = rows.shape[1]
    spec = pl.BlockSpec((EXPERTS, group, EXP_CAP, WIDTH), lambda i: (0, i, 0, 0))
    return pl.pallas_call(
        expert_kernel,
        grid=(count // group,),
        in_specs=[
            spec,
            pl.BlockSpec(w_in.shape, lambda i: (0, 0, 0), pipeline_mode=pl.Buffered(1)),
            pl.BlockSpec(w_down.shape, lambda i: (0, 0, 0), pipeline_mode=pl.Buffered(1)),
        ],
        out_specs=spec,
        out_shape=pltpu.MemorySpace.HBM(rows.shape, jnp.bfloat16),
        scratch_shapes=[
            pltpu.VMEM((group * EXP_CAP, width), jnp.float32),
            pltpu.VMEM((group * EXP_CAP, width), jnp.bfloat16),
        ],
        compiler_params=pltpu.CompilerParams(vmem_limit_bytes=63 * MIB),
        cost_estimate=pl.CostEstimate(flops=2 * 512 * 512 * width, bytes_accessed=12 * MIB, transcendentals=256 * 512),
    )(in_hbm(rows), in_hbm(w_in), in_hbm(w_down))


def attend(query, k, v):
    heads = query.shape[1] // HEAD_DIM
    chip, core = lax.axis_index("z"), lax.axis_index("core")
    q = query.reshape(BLOCK, heads, HEAD_DIM)
    k = k.reshape(-1, HEAD_DIM)
    v = v.reshape(-1, HEAD_DIM)
    scores = jnp.einsum("qhd,kd->hqk", q, k, preferred_element_type=jnp.float32)
    scores = scores / math.sqrt(HEAD_DIM)
    place = jnp.arange(k.shape[0])
    key_core = jnp.where(place < Z * BLOCK, core, 1 - core)
    key_pos = (place // BLOCK % Z * 2 + key_core) * BLOCK + place % BLOCK
    query_pos = (chip * 2 + core) * BLOCK + jnp.arange(BLOCK)
    causal = query_pos[:, None] >= key_pos[None, :]
    scores = jnp.where(causal[None], scores, -1e30)
    top = jnp.max(scores, axis=-1, keepdims=True)
    raised = jnp.exp(scores - top)
    probs = (raised / jnp.sum(raised, axis=-1, keepdims=True)).astype(jnp.bfloat16)
    out = jnp.einsum("hqk,kd->qhd", probs, v, preferred_element_type=jnp.float32)
    return out.reshape(BLOCK, heads * HEAD_DIM)


def ranks_of(ids):
    grid = jnp.arange(EXPERTS, dtype=jnp.int32)
    picked = ids[:, :, None] == grid[None, None, :]
    chosen = jnp.any(picked, axis=1)
    rows = ids.shape[0]
    lower = (jnp.arange(rows)[:, None] > jnp.arange(rows)[None, :]).astype(jnp.bfloat16)
    rank = jnp.dot(lower, chosen.astype(jnp.bfloat16), preferred_element_type=jnp.float32).astype(jnp.int32)
    return jnp.sum(jnp.where(picked, rank[:, None, :], 0), axis=2)


def swap_columns(x):
    return lax.all_to_all(x, E, split_axis=0, concat_axis=0, tiled=True)


def per_device(query, keys, values, resid, route_ids, route_weight, w_in, w_down):
    w_in = lax.all_gather(w_in, "core", axis=0, tiled=True)
    w_down = lax.all_gather(w_down, "core", axis=0, tiled=True)
    k, v = gather_kv(keys, values)
    attended = attend(query, k, v)
    state = (resid.astype(jnp.float32) + attended).astype(jnp.bfloat16)

    ranks = ranks_of(route_ids)
    gates = route_weight / jnp.sum(route_weight, axis=1, keepdims=True)
    sent = jnp.concatenate([state, notes_of(route_ids, ranks, gates)], axis=0)
    plane = lax.all_gather(sent, "z", axis=0)
    plane_slots, plane_gates = read_notes(plane[:, BLOCK:])
    slots_t, gates_t = plane_slots.transpose(0, 2, 1), plane_gates.transpose(0, 2, 1)
    rows = [swap_columns(place_rows(plane, part)) for part in range(PARTS)]
    outs = [experts(part, w_in, w_down) for part in rows]
    outs[0], rows[1] = lax.optimization_barrier((outs[0], rows[1]))
    mixes = [mix_rows(slots_t, gates_t, swap_columns(out), part) for part, out in enumerate(outs)]
    mix = swap_chips(jnp.concatenate(mixes, axis=0))
    mixture = jnp.sum(mix.astype(jnp.float32), axis=0)
    return (state.astype(jnp.float32) + mixture).astype(jnp.bfloat16)


def solution(mesh):
    fine = Mesh(mesh.devices.reshape(4, 4, 16, 2), ("x", "y", "z", "core"))
    placed = (
        P(T, E),
        P(T, None),
        P(T, None),
        P(T, E),
        P(T, None),
        P(T, None),
        P(E, None, T),
        P(E, T, None),
    )
    return jax.shard_map(per_device, mesh=fine, in_specs=placed, out_specs=P(T, E), check_vma=False)
```
